256 devices in a mesh: rows: 64 (over x, z, core), rhs: 4 (over y).
Axes of the slice: x: 4, y: 4, z: 8, core: 2. Of those that a mesh axis runs over, the one named last changes fastest.
Arguments:
- right_sides: float32 [4, 65536, 512], P(None, 'rows', 'rhs'), may hold values from -6 to 6
- butterfly_diagonals: float32 [2, 4, 65536], P(None, None, 'rows'), may hold values from 0.5 to 2
- band_rows: float32 [1024, 4, 65536], P(None, None, ('rows', 'rhs')), may hold values from -0.1875 to 0.1875
- diag_inverse: float32 [1024, 1024], replicated, as said below
- band_block: int32 [1], replicated, may hold values from 0 to 254
Outputs:
- updated_sides: float32 [4, 65536, 512], P(None, 'rows', 'rhs')
The draws below stay inside these ranges and needn't reach their ends.
Inputs may be any that keep to these rules, and one draw needn't show every extreme that they name: `diag_inverse`: upper triangular with diagonal entries between 0.5 and 1.
All inputs are finite; a program needn't handle non-finite values.
Results may differ from the reference program's by a relative error of at most 0.000082.
Values sent between devices are 32-bit elements; how exact they have to be, the bound alone decides.
No kernel may reach another device: no remote copies, remote signals or barrier semaphores. Data moves between devices by JAX's collectives and lax.ppermute only.
A program may use at most 128 MiB of HBM per device.

```python
import math
import jax
import jax.numpy as jnp
from jax import lax

NB = 1024
NRHS = 512
CYC = 4
N_ROWS = 64


def draw_diag_inverse(key, part):
    key = jax.random.fold_in(key, 5)
    first, second = jax.random.split(key)
    above = jax.random.normal(first, (NB, NB), jnp.float32) * (0.5 / jnp.sqrt(jnp.float32(NB)))
    middle = jax.random.uniform(second, (NB,), jnp.float32, 0.5, 1.0)
    row_index = jnp.arange(NB)[:, None]
    col_index = jnp.arange(NB)[None, :]
    return jnp.where(col_index > row_index, above, 0.0) + jnp.diag(middle)


def block_scale(own_key, shape, shards, smallest, high):
    def one(dim, shards_of):
        heights = jax.random.uniform(jax.random.fold_in(jax.random.fold_in(own_key, 6), dim), (shards_of,), jnp.float32, smallest / len(shards), high / len(shards))
        return jnp.repeat(jnp.exp(heights), shape[dim] // shards_of).reshape((-1,) + (1,) * (len(shape) - dim - 1))

    level = one(*shards[0])
    for cut in shards[1:]:
        level = level * one(*cut)
    return level


def normal_values(rng, shape, width, bound, shards=(), kind=jnp.bfloat16):
    factor_of = block_scale(rng, shape, shards, -0.22, 0.18) if shards else 1.0
    values = jax.random.normal(rng, shape, jnp.float32) * width * factor_of
    return jnp.minimum(jnp.maximum(values, -bound), bound).astype(kind)


def setup_inputs(seed: int = 0) -> dict:
    key_of = jax.random.split(jax.random.key(seed), 6)
    return {
        "right_sides": normal_values(key_of[0], (CYC, N_ROWS * NB, NRHS), 1.0, 6.0, ((1, 64), (2, 4)), jnp.float32),
        "butterfly_diagonals": jnp.clip(jnp.exp(math.log(2.0) - 1.3862944 * jax.random.uniform(key_of[1], (2, CYC, N_ROWS * NB), jnp.float32) ** block_scale(key_of[1], (2, CYC, N_ROWS * NB), ((2, 64),), -0.2, 0.2)), 0.5, 2.0),
        "band_rows": normal_values(key_of[2], (NB, CYC, N_ROWS * NB), NB ** -0.5, 0.1875, ((2, 256),), jnp.float32),
        "diag_inverse": draw_diag_inverse(jax.random.fold_in(key_of[5], 71), 0),
        "band_block": jax.random.randint(key_of[4], (1,), 0, CYC * N_ROWS - 1).astype(jnp.int32),
    }


def apply_level(values, coefs, half):
    blocks = N_ROWS // (2 * half)
    shaped = values.reshape(CYC, blocks, 2, half * NB, NRHS)
    scales = coefs.reshape(CYC, blocks, 2, half * NB, 1)
    upper = shaped[:, :, 0]
    lower = shaped[:, :, 1]
    factor = 1.0 / jnp.sqrt(jnp.float32(2.0))
    new_upper = scales[:, :, 0] * (upper + lower) * factor
    new_lower = scales[:, :, 1] * (upper - lower) * factor
    return jnp.stack([new_upper, new_lower], axis=2).reshape(CYC, N_ROWS * NB, NRHS)

def reference(right_sides, butterfly_diagonals, band_rows, diag_inverse, band_block):
    moved = apply_level(right_sides, butterfly_diagonals[0], N_ROWS // 2)
    moved = apply_level(moved, butterfly_diagonals[1], N_ROWS // 4)
    start = band_block[0].astype(jnp.int32)
    blocks = moved.reshape(CYC * N_ROWS, NB, NRHS)
    band_rhs = lax.dynamic_index_in_dim(blocks, start, 0, keepdims=False)
    solved = jnp.dot(diag_inverse.T, band_rhs, precision=lax.Precision.HIGHEST, preferred_element_type=jnp.float32)
    flat_rows = band_rows.reshape(NB, CYC * N_ROWS * NB)
    update = jnp.dot(flat_rows.T, solved, precision=lax.Precision.HIGHEST, preferred_element_type=jnp.float32)
    update = update.reshape(CYC * N_ROWS, NB, NRHS)
    index = jnp.arange(CYC * N_ROWS, dtype=jnp.int32)[:, None, None]
    result = jnp.where(index == start, solved[None], jnp.where(index > start, blocks - update, blocks))
    return result.reshape(CYC, N_ROWS * NB, NRHS)
```

```python
import functools
import jax
import jax.numpy as jnp
from jax import lax
from jax.experimental import pallas as pl
from jax.experimental.pallas import tpu as pltpu
from jax.sharding import PartitionSpec as P

NX, NZ, NC, NY = 4, 8, 2, 4
NB = 1024
HALF = 16
F32 = jnp.float32
BF16 = jnp.bfloat16


def row_perm(move):
    pairs = []
    for x in range(NX):
        for z in range(NZ):
            for c in range(NC):
                a, b, d = move(x, z, c)
                pairs.append(((x * NZ + z) * NC + c, ((a % NX) * NZ + b % NZ) * NC + d))
    return pairs


def shift_x(v, s):
    return lax.ppermute(v, "rows", row_perm(lambda x, z, c: (x + s, z, c)))


def shift_z(v, s):
    return lax.ppermute(v, "rows", row_perm(lambda x, z, c: (x, z + s, c)))


def other_core(v):
    return lax.ppermute(v, "rows", row_perm(lambda x, z, c: (x, z, 1 - c)))


def shift_y(v, s):
    return lax.ppermute(v, "rhs", [(i, (i + s) % NY) for i in range(NY)])


X_GROUPS = [[(x * NZ + z) * NC + c for x in range(NX)] for z in range(NZ) for c in range(NC)]


def exchange_x(v):
    return lax.all_to_all(v, "rows", 0, 0, axis_index_groups=X_GROUPS, tiled=True)


def params(mib):
    return pltpu.CompilerParams(vmem_limit_bytes=mib << 20)


def prep_kernel(info, slab, diag, out):
    cycle = info[0] // (NX * NZ * NC)
    flipped = slab[0].T
    for i in range(NX):
        out[i, :32, :] = flipped[32 * i : 32 * i + 32]
        out[i, 32:33, :] = diag[0, pl.ds(cycle, 1), :]
        out[i, 33:34, :] = diag[1, pl.ds(cycle, 1), :]
        out[i, 34:40, :] = jnp.zeros((6, NB), F32)


def prep(info, right_sides, diag):
    return pl.pallas_call(
        prep_kernel,
        grid_spec=pltpu.PrefetchScalarGridSpec(
            num_scalar_prefetch=1,
            grid=(1,),
            in_specs=[
                pl.BlockSpec((1, NB, 128), lambda i, s: (s[0] // (NX * NZ * NC), 0, 0)),
                pl.BlockSpec((2, 4, NB), lambda i, s: (0, 0, 0)),
            ],
            out_specs=pl.BlockSpec((NX, 40, NB), lambda i, s: (0, 0, 0)),
        ),
        out_shape=jax.ShapeDtypeStruct((NX, 40, NB), F32),
        compiler_params=params(16),
        name="prep",
    )(info, right_sides, diag)


def solve_kernel(info, got, inverse, out):
    x0 = info[0] % (NX * NZ * NC) // (NZ * NC)
    high = x0 & 2
    sign_high = jnp.where(high == 0, 1.0, -1.0).astype(F32)
    sign_low = jnp.where((x0 & 1) == 0, 1.0, -1.0).astype(F32)
    level = [
        got[high | p, 32:33, :] * (got[p, :32, :] + sign_high * got[p + 2, :32, :])
        for p in range(2)
    ]
    sides = got[x0, 33:34, :] * (0.5 * (level[0] + sign_low * level[1]))
    out[...] = jnp.dot(
        sides, inverse[...], precision=lax.Precision.HIGHEST, preferred_element_type=F32
    )


def solve(info, got, inverse):
    return pl.pallas_call(
        solve_kernel,
        grid_spec=pltpu.PrefetchScalarGridSpec(
            num_scalar_prefetch=1,
            grid=(4,),
            in_specs=[
                pl.BlockSpec((NX, 40, NB), lambda i, s: (0, 0, 0)),
                pl.BlockSpec((NB, 256), lambda i, s: (0, i)),
            ],
            out_specs=pl.BlockSpec((32, 256), lambda i, s: (0, i)),
        ),
        out_shape=jax.ShapeDtypeStruct((32, NB), F32),
        compiler_params=params(24),
        name="solve",
    )(info, got, inverse)


def split(v):
    top = v.astype(BF16)
    return top, (v - top.astype(F32)).astype(BF16)


def band_kernel(rows, top, low):
    for c in range(4):
        a, b = split(rows[:, c, :])
        top[c] = a
        low[c] = b


def split_band(band_rows):
    spec = pl.BlockSpec((4, 256, 256), lambda i: (0, i, 0))
    shape = jax.ShapeDtypeStruct((4, NB, 256), BF16)
    return pl.pallas_call(
        band_kernel,
        grid=(4,),
        in_specs=[pl.BlockSpec((256, 4, 256), lambda i: (i, 0, 0))],
        out_specs=[spec, spec],
        out_shape=[shape, shape],
        compiler_params=params(24),
        name="split_band",
    )(band_rows)


def update_kernel(info, *refs):
    own, other = refs[0:4], refs[4:8]
    top, low = refs[8:10]
    outs, mine = refs[10:14], refs[14]
    left_top, left_low = refs[15:17]

    @pl.when(pl.program_id(0) == 0)
    def _():
        x, core = info[1], info[3]
        for t in range(NX):
            for h in range(NC):
                base = 32 * ((x - t + NX) % NX) + HALF * (core ^ h)
                for s in range(NY):
                    piece = (other if h else own)[t][HALF * s : HALF * s + HALF, :]
                    a, b = split(piece)
                    at = pl.ds(pl.multiple_of(128 * s + base, HALF), HALF)
                    left_top[at, :] = a
                    left_low[at, :] = b
                    if s == 0:
                        mine[pl.ds(pl.multiple_of(base, HALF), HALF), :] = piece

    for s in range(NY):
        at = slice(128 * s, 128 * s + 128)
        outs[s][...] = (
            jnp.dot(left_top[at, :], low[0], preferred_element_type=F32)
            + jnp.dot(left_low[at, :], top[0], preferred_element_type=F32)
            + jnp.dot(left_top[at, :], top[0], preferred_element_type=F32)
        )


def update(info, own, other, top, low):
    whole = pl.BlockSpec((64, NB), lambda i, s: (0, 0))
    band = pl.BlockSpec((1, NB, 256), lambda i, s: (i, 0, 0))
    part = pl.BlockSpec((128, 256), lambda i, s: (0, i))
    shape = jax.ShapeDtypeStruct((128, NB), F32)
    return pl.pallas_call(
        update_kernel,
        grid_spec=pltpu.PrefetchScalarGridSpec(
            num_scalar_prefetch=1,
            grid=(4,),
            in_specs=[whole] * 8 + [band] * 2,
            out_specs=[part] * 4 + [pl.BlockSpec((128, NB), lambda i, s: (0, 0))],
            scratch_shapes=[pltpu.VMEM((512, NB), BF16)] * 2,
        ),
        out_shape=[shape] * 5,
        compiler_params=params(32),
        name="update",
    )(info, *own, *other, top, low)


def mid_kernel(got, out):
    level1 = [got[j, NB : NB + 8, :].T for j in range(NX)]
    level2 = [0.5 * got[j, NB + 8 : NB + 16, :].T for j in range(NX)]
    for i in range(NB // 128):
        at = slice(128 * i, 128 * i + 128)
        a, b, c, d = [got[j, at, :] for j in range(NX)]
        first = [a + c, b + d, a - c, b - d]
        first = [level1[j][:, i : i + 1] * first[j] for j in range(NX)]
        a, b, c, d = first
        second = [a + b, a - b, c + d, c - d]
        for j in range(NX):
            out[j, at, :] = level2[j][:, i : i + 1] * second[j]


def mid(got):
    return pl.pallas_call(
        mid_kernel,
        out_shape=jax.ShapeDtypeStruct((NX, NB, 128), F32),
        compiler_params=params(24),
        name="mid",
    )(got)


def last_kernel(info, moved, mine, *refs):
    parts, out = refs[:4], refs[4]
    start, x, z, core, y = [info[i] for i in range(5)]
    index = pl.program_id(0) * (NX * NZ * NC) + (x * NZ + z) * NC + core

    @pl.when(index < start)
    def _():
        out[...] = moved[...]

    @pl.when(index == start)
    def _():
        out[0] = mine[...].T

    @pl.when(index > start)
    def _():
        for s in range(NY):
            at = pl.ds(pl.multiple_of(256 * ((y + s) % NY), 256), 256)
            out[0, at, :] = moved[0, at, :] - parts[s][...].T


def last(info, moved, mine, parts):
    block = pl.BlockSpec((1, NB, 128), lambda i, s: (i, 0, 0))
    return pl.pallas_call(
        last_kernel,
        grid_spec=pltpu.PrefetchScalarGridSpec(
            num_scalar_prefetch=1,
            grid=(4,),
            in_specs=[block, pl.BlockSpec((128, NB), lambda i, s: (0, 0))]
            + [pl.BlockSpec((128, 256), lambda i, s: (0, i))] * 4,
            out_specs=block,
        ),
        out_shape=jax.ShapeDtypeStruct((4, NB, 128), F32),
        compiler_params=params(24),
        name="last",
    )(info, moved, mine, *parts)


def per_device(right_sides, butterfly_diagonals, band_rows, diag_inverse, band_block):
    place = lax.axis_index("rows")
    y = lax.axis_index("rhs")
    x, z, core = place // (NZ * NC), place // NC % NZ, place % NC
    start = band_block[0]
    info = jnp.stack([start, x, z, core, y]).astype(jnp.int32)
    z0 = start % (NX * NZ * NC) // NC % NZ
    core0 = start % NC

    message = prep(info, right_sides, butterfly_diagonals)
    got = exchange_x(message)
    packed = jnp.concatenate(
        [right_sides, butterfly_diagonals.transpose(1, 0, 2).reshape(4, 16, 128)], axis=1
    )
    packed = lax.optimization_barrier((packed, message))[0]
    mixed = exchange_x(packed)
    top, low = split_band(band_rows)

    piece = solve(info, got, diag_inverse)
    halves = piece.reshape(NC, HALF, NB)
    from_other = other_core(lax.dynamic_index_in_dim(halves, 1 - core, 0, keepdims=False))
    half = jnp.where(core == core0, lax.dynamic_index_in_dim(halves, core, 0, keepdims=False), from_other)

    ahead = (z - z0) % NZ
    up, down = shift_z(half, 1), shift_z(half, -1)
    half = jnp.where(ahead == 1, up, jnp.where(ahead == NZ - 1, down, half))
    up, down = shift_z(half, 3), shift_z(half, -3)
    half = jnp.where(
        (ahead >= 2) & (ahead <= 4), up, jnp.where((ahead == 5) | (ahead == 6), down, half)
    )

    line = jnp.concatenate([half] + [shift_y(half, s) for s in range(1, NY)], axis=0)
    own = [line] + [shift_x(line, t) for t in range(1, NX)]
    other = [other_core(v) for v in own]

    parts = update(info, own, other, top, low)
    mine = parts[4]
    parts = [parts[0]] + [shift_y(parts[s], -s) for s in range(1, NY)]
    moved = exchange_x(mid(mixed))
    return last(info, moved, mine, parts)


def solution(mesh):
    return jax.shard_map(
        per_device,
        mesh=mesh,
        in_specs=(
            P(None, "rows", "rhs"),
            P(None, None, "rows"),
            P(None, None, ("rows", "rhs")),
            P(),
            P(),
        ),
        out_specs=P(None, "rows", "rhs"),
        check_vma=False,
    )
```

```python
import functools
import jax
import jax.numpy as jnp
from jax import lax
from jax.experimental import pallas as pl
from jax.experimental.pallas import tpu as pltpu
from jax.sharding import PartitionSpec as P

NX, NZ, NC, NY = 4, 8, 2, 4
NB = 1024
HALF = 16
F32 = jnp.float32
BF16 = jnp.bfloat16


def row_perm(move):
    pairs = []
    for x in range(NX):
        for z in range(NZ):
            for c in range(NC):
                a, b, d = move(x, z, c)
                pairs.append(((x * NZ + z) * NC + c, ((a % NX) * NZ + b % NZ) * NC + d))
    return pairs


def flip_x(v, m):
    return lax.ppermute(v, "rows", row_perm(lambda x, z, c: (x ^ m, z, c))) if m else v


def flip_z(v, m):
    return lax.ppermute(v, "rows", row_perm(lambda x, z, c: (x, z ^ m, c)))


def flip_y(v, m):
    return lax.ppermute(v, "rhs", [(i, i ^ m) for i in range(NY)]) if m else v


X_GROUPS = [[(x * NZ + z) * NC + c for x in range(NX)] for z in range(NZ) for c in range(NC)]


def exchange_x(v):
    return lax.all_to_all(v, "rows", 0, 0, axis_index_groups=X_GROUPS, tiled=True)


def other_core(v):
    return lax.ppermute(v, "rows", row_perm(lambda x, z, c: (x, z, 1 - c)))


def far(*values):
    return [pltpu.with_memory_space_constraint(v, pltpu.HBM) for v in values]


def params(mib):
    return pltpu.CompilerParams(vmem_limit_bytes=mib << 20)


ANY = pl.BlockSpec(memory_space=pl.ANY)


def whole(*shape):
    return pl.BlockSpec(shape, lambda i, s: (0,) * len(shape))


def call(body, name, grid, info, args, in_specs, out_specs, out_shape, mib, scratch=(), hint=0):
    cost = pl.CostEstimate(flops=hint, bytes_accessed=1 << 20, transcendentals=0)
    return pl.pallas_call(
        body,
        grid_spec=pltpu.PrefetchScalarGridSpec(
            num_scalar_prefetch=1,
            grid=(grid,),
            in_specs=in_specs,
            out_specs=out_specs,
            scratch_shapes=list(scratch),
        ),
        out_shape=out_shape,
        compiler_params=params(mib),
        cost_estimate=cost if hint else None,
        name=name,
    )(info, *args)


def prep_kernel(info, slab, diag, *refs):
    outs, flipped = refs[:NX], refs[NX]
    cycle, x = info[0] // (NX * NZ * NC), info[1]
    flipped[...] = slab[0].T
    for s in range(NX):
        to = x ^ s
        outs[s][:32, :] = flipped[pl.ds(pl.multiple_of(32 * to, 32), 32), :]
        for level in range(2):
            outs[s][32 + level : 33 + level, :] = diag[level, pl.ds(cycle, 1), :]
            outs[s][34 + level : 35 + level, :] = diag[level, pl.ds(to, 1), :]
        outs[s][36:40, :] = jnp.zeros((4, 256), F32)


def prep(info, right_sides, diag):
    return call(
        prep_kernel,
        "prep",
        4,
        info,
        far(right_sides, diag),
        [
            pl.BlockSpec((1, 256, 128), lambda i, s: (s[0] // (NX * NZ * NC), i, 0)),
            pl.BlockSpec((2, 4, 256), lambda i, s: (0, 0, i)),
        ],
        [pl.BlockSpec((40, 256), lambda i, s: (0, i))] * NX,
        [jax.ShapeDtypeStruct((40, NB), F32)] * NX,
        12,
        [pltpu.VMEM((128, 256), F32)],
    )


def split(v):
    top = v.astype(BF16)
    return top, (v - top.astype(F32)).astype(BF16)


TOKEN = jax.ShapeDtypeStruct((8, 128), F32)


def split_band_kernel(info, rows, token, top, low, mark):
    mark[...] = jnp.zeros((8, 128), F32)
    for c in range(4):
        for half in range(2):
            a, b = split(rows[pl.ds(4 * half + c, 256, stride=8), :])
            top[c, :, 128 * half : 128 * half + 128] = a
            low[c, :, 128 * half : 128 * half + 128] = b


def split_band(info, band_rows, token):
    view = band_rows.reshape(NB, 4, 2, 128).transpose(0, 2, 1, 3).reshape(8 * NB, 128)
    spec = pl.BlockSpec((4, 256, 256), lambda i, s: (0, i, 0))
    return call(
        split_band_kernel,
        "split_band",
        4,
        info,
        (view, token),
        [pl.BlockSpec((2048, 128), lambda i, s: (i, 0)), ANY],
        [spec, spec, whole(8, 128)],
        [pltpu.HBM((4, NB, 256), BF16)] * 2 + [TOKEN],
        12,
    )


def product(a, b):
    return jnp.dot(a, b, preferred_element_type=F32)


def solve_kernel(info, *refs):
    pieces, inverse = refs[:4], refs[4]
    keep, send, got, top, low, full = refs[6:]
    step = pl.program_id(0)
    x, core = info[1], info[3]

    @pl.when(step == 0)
    def _():
        for s in range(NX):
            got[x ^ s] = pieces[s][...]
        x0 = info[0] % (NX * NZ * NC) // (NZ * NC)
        high = x0 & 2
        sign_high = jnp.where(high == 0, 1.0, -1.0).astype(F32)
        sign_low = jnp.where((x0 & 1) == 0, 1.0, -1.0).astype(F32)
        level = [
            got[high | p, 32:33, :] * (got[p, :32, :] + sign_high * got[p + 2, :32, :])
            for p in range(2)
        ]
        top[...], low[...] = split(
            got[x0, 33:34, :] * (0.5 * (level[0] + sign_low * level[1]))
        )

    for i in range(4):

        @pl.when(step == i)
        def _():
            depth = 256 * (i + 1)
            a, b = split(inverse[:depth, :])
            full[...] = (
                product(top[:, :depth], b)
                + product(low[:, :depth], a)
                + product(top[:, :depth], a)
            )

    keep[...] = full[pl.ds(pl.multiple_of(HALF * core, HALF), HALF), :]
    send[...] = full[pl.ds(pl.multiple_of(HALF * (1 - core), HALF), HALF), :]


def solve(info, pieces, inverse, token):
    part = pl.BlockSpec((HALF, 256), lambda i, s: (0, i))
    return call(
        solve_kernel,
        "solve",
        4,
        info,
        (*pieces, *far(inverse), token),
        [whole(40, NB)] * NX + [pl.BlockSpec((NB, 256), lambda i, s: (0, i)), ANY],
        [part] * 2,
        [jax.ShapeDtypeStruct((HALF, NB), F32)] * 2,
        12,
        [
            pltpu.VMEM((NX, 40, NB), F32),
            pltpu.VMEM((32, NB), BF16),
            pltpu.VMEM((32, NB), BF16),
            pltpu.VMEM((32, 256), F32),
        ],
    )


def update_kernel(n, info, *refs):
    own, other = refs[:n], refs[n : 2 * n]
    top, low = refs[2 * n : 2 * n + 2]
    outs, mine = refs[2 * n + 3 : 3 * n + 3], refs[3 * n + 3]
    left = refs[3 * n + 4]
    rows = 128 * n

    @pl.when(pl.program_id(0) == 0)
    def _():
        x, core = info[1], info[3]
        for t in range(NX):
            for h in range(NC):
                base = 32 * (x ^ t) + HALF * (core ^ h)
                for s in range(n):
                    piece = (other if h else own)[s][HALF * t : HALF * t + HALF, :]
                    a, b = split(piece)
                    left[pl.ds(pl.multiple_of(128 * s + base, HALF), HALF), :] = a
                    left[pl.ds(pl.multiple_of(rows + 128 * s + base, HALF), HALF), :] = b
                    if s == 0:
                        mine[pl.ds(pl.multiple_of(base, HALF), HALF), :] = piece

    both = product(left[...], top[0])
    done = product(left[:rows, :], low[0]) + both[rows:] + both[:rows]
    for s in range(n):
        outs[s][...] = done[128 * s : 128 * s + 128]


def update(info, own, other, top, low, token):
    n = len(own)
    band = pl.BlockSpec((1, NB, 256), lambda i, s: (i, 0, 0))
    return call(
        functools.partial(update_kernel, n),
        "update",
        4,
        info,
        (*own, *other, *far(top, low), token),
        [whole(64, NB)] * (2 * n) + [band] * 2 + [ANY],
        [pl.BlockSpec((128, 256), lambda i, s: (0, i))] * n + [whole(128, NB)],
        [jax.ShapeDtypeStruct((128, NB), F32)] * (n + 1),
        12,
        [pltpu.VMEM((256 * n, NB), BF16)],
        1,
    )


def mid_kernel(info, *refs):
    got, pieces, outs, mark = refs[0], refs[1:5], refs[6:10], refs[10]
    mark[...] = jnp.zeros((8, 128), F32)
    x = info[1]
    high = [jnp.where((x ^ s) & 2 == 0, 1.0, -1.0).astype(F32) for s in range(NX)]
    low = [jnp.where((x ^ s) & 1 == 0, 1.0, -1.0).astype(F32) for s in range(NX)]
    for i in range(NB // 128):
        at = slice(128 * i, 128 * i + 128)
        scale = [pieces[s][:, at].T for s in range(NX)]
        v = [got[x ^ s, at, :] for s in range(NX)]
        v = [scale[s][:, 2:3] * (v[s ^ 2] + high[s] * v[s]) for s in range(NX)]
        for s in range(NX):
            outs[s][at, :] = (0.5 * scale[s][:, 3:4]) * (v[s ^ 1] + low[s] * v[s])


def mid(info, got, pieces, token):
    return call(
        mid_kernel,
        "mid",
        1,
        info,
        (got, *far(*pieces), token),
        [whole(NX, NB, 128)]
        + [pl.BlockSpec((8, NB), lambda i, s: (4, 0))] * NX
        + [ANY],
        [whole(NB, 128)] * NX + [whole(8, 128)],
        [jax.ShapeDtypeStruct((NB, 128), F32)] * NX + [TOKEN],
        12,
        hint=10**10,
    )


def last_kernel(info, *refs):
    moved, mine, parts, out = refs[:4], refs[4], refs[5:9], refs[9]
    start, x, z, core, y = [info[i] for i in range(5)]
    step = pl.program_id(0)
    index = (x ^ step) * (NX * NZ * NC) + (x * NZ + z) * NC + core

    for s in range(NX):

        @pl.when((step == s) & (index < start))
        def _():
            out[0] = moved[s][...]

        @pl.when((step == s) & (index > start))
        def _():
            for q in range(NY):
                at = pl.ds(pl.multiple_of(256 * (y ^ q), 256), 256)
                out[0, at, :] = moved[s][at, :] - parts[q][...].T

    @pl.when(index == start)
    def _():
        out[0] = mine[...].T


def last(info, moved, mine, parts):
    return call(
        last_kernel,
        "last",
        NX,
        info,
        (*moved, mine, *parts),
        [whole(NB, 128)] * NX
        + [whole(128, NB)]
        + [pl.BlockSpec((128, 256), lambda i, s: (0, s[1] ^ i))] * NY,
        pl.BlockSpec((1, NB, 128), lambda i, s: (s[1] ^ i, 0, 0)),
        jax.ShapeDtypeStruct((4, NB, 128), F32),
        12,
    )


def after(value, token):
    return lax.optimization_barrier((value, token))[0]


def per_device(right_sides, butterfly_diagonals, band_rows, diag_inverse, band_block):
    place = lax.axis_index("rows")
    y = lax.axis_index("rhs")
    x, z, core = place // (NZ * NC), place // NC % NZ, place % NC
    start = band_block[0]
    info = jnp.stack([start, x, z, core, y]).astype(jnp.int32)
    z0 = start % (NX * NZ * NC) // NC % NZ
    core0 = start % NC

    message = prep(info, right_sides, butterfly_diagonals)
    pieces = [flip_x(message[s], s) for s in range(NX)]
    top, low, ready = split_band(info, band_rows, message[0])
    mixed = exchange_x(after(right_sides, (pieces, ready)))

    half, other_half = solve(info, pieces, diag_inverse, ready)
    half = jnp.where(core == core0, half, other_core(other_half))

    away = z ^ z0
    got = [flip_z(half, m) for m in (1, 2, 3)]
    for m in (1, 2, 3):
        half = jnp.where(away == m, got[m - 1], half)
    half = jnp.where(away >= 4, flip_z(half, 6), half)

    line = jnp.concatenate([half] + [flip_x(half, t) for t in range(1, NX)], axis=0)
    own = [flip_y(line, s) for s in range(NY)]
    *blocks, mixed_done = mid(info, mixed, pieces, line)
    moved = [flip_x(v, s) for s, v in enumerate(blocks)]

    other = [other_core(after(v, mixed_done)) for v in own[1:]]
    one, two, three, token = update(info, own[1:], other, top, low, mixed_done)
    rest = after(own[0], moved)
    zero, mine = update(info, [rest], [other_core(rest)], top, low, token)
    parts = [zero, flip_y(one, 1), flip_y(two, 2), flip_y(three, 3)]
    return last(info, moved, mine, parts)


def solution(mesh):
    return jax.shard_map(
        per_device,
        mesh=mesh,
        in_specs=(
            P(None, "rows", "rhs"),
            P(None, None, "rows"),
            P(None, None, ("rows", "rhs")),
            P(),
            P(),
        ),
        out_specs=P(None, "rows", "rhs"),
        check_vma=False,
    )
```

```python
import functools
import jax
import jax.numpy as jnp
from jax import lax
from jax.experimental import pallas as pl
from jax.experimental.pallas import tpu as pltpu
from jax.sharding import PartitionSpec as P

NX, NZ, NC, NY = 4, 8, 2, 4
NB = 1024
HALF = 16
OWN_HINT = 2 * 10**9
F32 = jnp.float32
BF16 = jnp.bfloat16


def row_perm(move):
    pairs = []
    for x in range(NX):
        for z in range(NZ):
            for c in range(NC):
                a, b, d = move(x, z, c)
                pairs.append(((x * NZ + z) * NC + c, ((a % NX) * NZ + b % NZ) * NC + d))
    return pairs


def flip_x(v, m):
    return lax.ppermute(v, "rows", row_perm(lambda x, z, c: (x ^ m, z, c))) if m else v


def flip_z(v, m):
    return lax.ppermute(v, "rows", row_perm(lambda x, z, c: (x, z ^ m, c)))


def flip_y(v, m):
    return lax.ppermute(v, "rhs", [(i, i ^ m) for i in range(NY)]) if m else v


X_GROUPS = [[(x * NZ + z) * NC + c for x in range(NX)] for z in range(NZ) for c in range(NC)]


def exchange_x(v):
    return lax.all_to_all(v, "rows", 0, 0, axis_index_groups=X_GROUPS, tiled=True)


def other_core(v):
    return lax.ppermute(v, "rows", row_perm(lambda x, z, c: (x, z, 1 - c)))


def far(*values):
    return [pltpu.with_memory_space_constraint(v, pltpu.HBM) for v in values]


def params(mib):
    return pltpu.CompilerParams(vmem_limit_bytes=mib << 20)


ANY = pl.BlockSpec(memory_space=pl.ANY)


def whole(*shape):
    return pl.BlockSpec(shape, lambda i, s: (0,) * len(shape))


def call(body, name, grid, info, args, in_specs, out_specs, out_shape, mib, scratch=(), hint=0, aliases={}):
    cost = pl.CostEstimate(flops=hint, bytes_accessed=1 << 20, transcendentals=0)
    return pl.pallas_call(
        body,
        grid_spec=pltpu.PrefetchScalarGridSpec(
            num_scalar_prefetch=1,
            grid=(grid,),
            in_specs=in_specs,
            out_specs=out_specs,
            scratch_shapes=list(scratch),
        ),
        out_shape=out_shape,
        input_output_aliases=aliases,
        compiler_params=params(mib),
        cost_estimate=cost if hint else None,
        name=name,
    )(info, *args)


def prep_kernel(info, slab, diag, *refs):
    outs, flipped = refs[:NX], refs[NX]
    cycle, x = info[0] // (NX * NZ * NC), info[1]
    flipped[...] = slab[0].T
    for s in range(NX):
        to = x ^ s
        outs[s][:32, :] = flipped[pl.ds(pl.multiple_of(32 * to, 32), 32), :]
        for level in range(2):
            outs[s][32 + level : 33 + level, :] = diag[level, pl.ds(cycle, 1), :]
            outs[s][34 + level : 35 + level, :] = diag[level, pl.ds(to, 1), :]
        outs[s][36:40, :] = jnp.zeros((4, 256), F32)


def prep(info, right_sides, diag):
    return call(
        prep_kernel,
        "prep",
        4,
        info,
        far(right_sides, diag),
        [
            pl.BlockSpec((1, 256, 128), lambda i, s: (s[0] // (NX * NZ * NC), i, 0)),
            pl.BlockSpec((2, 4, 256), lambda i, s: (0, 0, i)),
        ],
        [pl.BlockSpec((40, 256), lambda i, s: (0, i))] * NX,
        [jax.ShapeDtypeStruct((40, NB), F32)] * NX,
        12,
        [pltpu.VMEM((128, 256), F32)],
    )


def split(v):
    top = v.astype(BF16)
    return top, (v - top.astype(F32)).astype(BF16)


TOKEN = jax.ShapeDtypeStruct((8, 128), F32)


def split_band_kernel(info, rows, token, top, low, mark, near, near_top, near_low, came, went):
    mark[...] = jnp.zeros((8, 128), F32)
    copies = []
    for i in range(4):
        part = pl.ds(2048 * i, 2048)
        copies.append(pltpu.make_async_copy(rows.at[part], near.at[part], came.at[i]))
        copies[i].start()
    sent = []
    for i in range(4):
        copies[i].wait()
        part = slice(256 * i, 256 * i + 256)
        for c in range(4):
            for half in range(2):
                a, b = split(near[pl.ds(2048 * i + 4 * half + c, 256, stride=8), :])
                at = slice(256 * c + 128 * half, 256 * c + 128 * half + 128)
                near_top[part, at] = a
                near_low[part, at] = b
        part = pl.ds(256 * i, 256)
        for j, (here, there) in enumerate(((near_top, top), (near_low, low))):
            sent.append(pltpu.make_async_copy(here.at[part], there.at[part], went.at[j, i]))
            sent[-1].start()
    for copy in sent:
        copy.wait()


def split_band(info, band_rows, token):
    view = band_rows.reshape(NB, 4, 2, 128).transpose(0, 2, 1, 3).reshape(8 * NB, 128)
    return call(
        split_band_kernel,
        "split_band",
        1,
        info,
        (*far(view), token),
        [ANY] * 2,
        [ANY] * 2 + [whole(8, 128)],
        [pltpu.HBM((NB, NB), BF16)] * 2 + [TOKEN],
        12,
        [
            pltpu.VMEM((8 * NB, 128), F32),
            pltpu.VMEM((NB, NB), BF16),
            pltpu.VMEM((NB, NB), BF16),
            pltpu.SemaphoreType.DMA((4,)),
            pltpu.SemaphoreType.DMA((2, 4)),
        ],
    )


def product(a, b):
    return jnp.dot(a, b, preferred_element_type=F32)


def solve_kernel(info, *refs):
    pieces, inverse = refs[:4], refs[4]
    keep, send, got, near, full, done = refs[6:]
    copies = []
    for i in range(4):
        part = (pl.ds(0, 256 * (i + 1)), pl.ds(256 * i, 256))
        copies.append(pltpu.make_async_copy(inverse.at[part], near.at[part], done.at[i]))
        copies[i].start()
    x, core = info[1], info[3]
    for s in range(NX):
        got[x ^ s] = pieces[s][...]
    x0 = info[0] % (NX * NZ * NC) // (NZ * NC)
    high = x0 & 2
    sign_high = jnp.where(high == 0, 1.0, -1.0).astype(F32)
    sign_low = jnp.where((x0 & 1) == 0, 1.0, -1.0).astype(F32)
    level = [
        got[high | p, 32:33, :] * (got[p, :32, :] + sign_high * got[p + 2, :32, :])
        for p in range(2)
    ]
    top, low = split(got[x0, 33:34, :] * (0.5 * (level[0] + sign_low * level[1])))
    for i in range(4):
        depth, at = 256 * (i + 1), slice(256 * i, 256 * i + 256)
        copies[i].wait()
        a, b = split(near[:depth, at])
        full[:, at] = (
            product(top[:, :depth], b) + product(low[:, :depth], a) + product(top[:, :depth], a)
        )
    keep[...] = full[pl.ds(pl.multiple_of(HALF * core, HALF), HALF), :]
    send[...] = full[pl.ds(pl.multiple_of(HALF * (1 - core), HALF), HALF), :]


def solve(info, pieces, inverse, token):
    return call(
        solve_kernel,
        "solve",
        1,
        info,
        (*pieces, *far(inverse), token),
        [whole(40, NB)] * NX + [ANY] * 2,
        [whole(HALF, NB)] * 2,
        [jax.ShapeDtypeStruct((HALF, NB), F32)] * 2,
        12,
        [
            pltpu.VMEM((NX, 40, NB), F32),
            pltpu.VMEM((NB, NB), F32),
            pltpu.VMEM((32, NB), F32),
            pltpu.SemaphoreType.DMA((4,)),
        ],
        70 * 10**9,
    )


def update_kernel(n, info, *refs):
    own, other = refs[:n], refs[n : 2 * n]
    far_top, far_low = refs[2 * n : 2 * n + 2]
    outs, mine = refs[2 * n + 3 : 3 * n + 3], refs[3 * n + 3]
    left_top, left_low, top, low, done = refs[3 * n + 4 :]
    copies = []
    for c in range(2):
        at = (slice(None), pl.ds(512 * c, 512))
        copies.append(
            [
                pltpu.make_async_copy(far_top.at[at], top.at[at], done.at[0, c]),
                pltpu.make_async_copy(far_low.at[at], low.at[at], done.at[1, c]),
            ]
        )
        for copy in copies[c]:
            copy.start()
    x, core = info[1], info[3]
    for t in range(NX):
        for h in range(NC):
            base = 32 * (x ^ t) + HALF * (core ^ h)
            for s in range(n):
                piece = (other if h else own)[s][HALF * t : HALF * t + HALF, :]
                at = pl.ds(pl.multiple_of(128 * s + base, HALF), HALF)
                left_top[at, :], left_low[at, :] = split(piece)
                if s == 0:
                    mine[pl.ds(pl.multiple_of(base, HALF), HALF), :] = piece
    for c in range(2):
        for copy in copies[c]:
            copy.wait()
        at = slice(512 * c, 512 * c + 512)
        result = (
            product(left_top[...], low[:, at])
            + product(left_low[...], top[:, at])
            + product(left_top[...], top[:, at])
        )
        for s in range(n):
            outs[s][:, at] = result[128 * s : 128 * s + 128]


def update(info, own, other, top, low, token, hint):
    n = len(own)
    return call(
        functools.partial(update_kernel, n),
        "update",
        1,
        info,
        (*own, *other, *far(top, low), token),
        [whole(64, NB)] * (2 * n) + [ANY] * 3,
        [whole(128, NB)] * (n + 1),
        [jax.ShapeDtypeStruct((128, NB), F32)] * (n + 1),
        20,
        [
            pltpu.VMEM((128 * n, NB), BF16),
            pltpu.VMEM((128 * n, NB), BF16),
            pltpu.VMEM((NB, NB), BF16),
            pltpu.VMEM((NB, NB), BF16),
            pltpu.SemaphoreType.DMA((2, 2)),
        ],
        hint,
    )


def mid_kernel(info, *refs):
    got, pieces, outs, mark = refs[0], refs[1:5], refs[6:10], refs[10]
    mark[...] = jnp.zeros((8, 128), F32)
    x = info[1]
    high = [jnp.where((x ^ s) & 2 == 0, 1.0, -1.0).astype(F32) for s in range(NX)]
    low = [jnp.where((x ^ s) & 1 == 0, 1.0, -1.0).astype(F32) for s in range(NX)]
    for i in range(NB // 128):
        at = slice(128 * i, 128 * i + 128)
        scale = [pieces[s][:, at].T for s in range(NX)]
        v = [got[x ^ s, at, :] for s in range(NX)]
        v = [scale[s][:, 2:3] * (v[s ^ 2] + high[s] * v[s]) for s in range(NX)]
        for s in range(NX):
            outs[s][at, :] = (0.5 * scale[s][:, 3:4]) * (v[s ^ 1] + low[s] * v[s])


def mid(info, got, pieces, token):
    return call(
        mid_kernel,
        "mid",
        1,
        info,
        (got, *far(*pieces), token),
        [whole(NX, NB, 128)]
        + [pl.BlockSpec((8, NB), lambda i, s: (4, 0))] * NX
        + [ANY],
        [whole(NB, 128)] * NX + [whole(8, 128)],
        [jax.ShapeDtypeStruct((NB, 128), F32)] * NX + [TOKEN],
        12,
        hint=10**10,
    )


def block_index(info, step):
    return ((info[1] ^ step) * NX + info[1]) * (NZ * NC) + info[2] * NC + info[3]


def last_kernel(info, *refs):
    moved, mine, parts, out = refs[:4], refs[4], refs[5:9], refs[9]
    step = pl.program_id(0)
    start, index = info[0], block_index(info, step)

    for s in range(NX):

        @pl.when((step == s) & (index < start))
        def _():
            out[0] = moved[s][...]

        @pl.when((step == s) & (index > start))
        def _():
            for q in range(NY):
                at = pl.ds(pl.multiple_of(256 * (info[4] ^ q), 256), 256)
                out[0, at, :] = moved[s][at, :] - parts[q][...].T

    @pl.when(index == start)
    def _():
        out[0] = mine[...].T


def last(info, moved, mine, parts):
    return call(
        last_kernel,
        "last",
        NX,
        info,
        (*moved, mine, *parts),
        [whole(NB, 128)] * NX
        + [whole(128, NB)]
        + [pl.BlockSpec((128, 256), lambda i, s: (0, s[1] ^ i))] * NY,
        pl.BlockSpec((1, NB, 128), lambda i, s: (s[1] ^ i, 0, 0)),
        jax.ShapeDtypeStruct((4, NB, 128), F32),
        12,
    )


def after(value, token):
    return lax.optimization_barrier((value, token))[0]


def per_device(right_sides, butterfly_diagonals, band_rows, diag_inverse, band_block):
    place = lax.axis_index("rows")
    y = lax.axis_index("rhs")
    x, z, core = place // (NZ * NC), place // NC % NZ, place % NC
    start = band_block[0]
    info = jnp.stack([start, x, z, core, y]).astype(jnp.int32)
    z0 = start % (NX * NZ * NC) // NC % NZ
    core0 = start % NC

    message = prep(info, right_sides, butterfly_diagonals)
    pieces = [flip_x(message[s], s) for s in range(NX)]
    top, low, ready = split_band(info, band_rows, message[0])
    mixed = exchange_x(after(right_sides, ready))

    half, other_half = solve(info, pieces, diag_inverse, ready)
    half = jnp.where(core == core0, half, other_core(other_half))

    away = z ^ z0
    got = [flip_z(half, m) for m in (1, 2, 3)]
    for m in (1, 2, 3):
        half = jnp.where(away == m, got[m - 1], half)
    half = jnp.where(away >= 4, flip_z(half, 6), half)

    line = jnp.concatenate([half] + [flip_x(half, t) for t in range(1, NX)], axis=0)
    *blocks, mixed_done = mid(info, mixed, pieces, line)
    moved = [flip_x(v, s) for s, v in enumerate(blocks)]

    one, three = flip_y(line, 1), flip_y(line, 3)
    two = flip_y(after(line, (one, three, mixed_done)), 2)
    cross = [other_core(after(v, mixed_done)) for v in (one, three)]
    one, three, token = update(info, [one, three], cross, top, low, mixed_done, 1)
    two = after(two, token)
    two, token = update(info, [two], [other_core(two)], top, low, token, 1)
    line = after(line, moved)
    zero, mine = update(info, [line], [other_core(line)], top, low, token, OWN_HINT)
    parts = [zero, flip_y(one, 1), flip_y(two, 2), flip_y(three, 3)]
    return last(info, moved, mine, parts)


def solution(mesh):
    return jax.shard_map(
        per_device,
        mesh=mesh,
        in_specs=(
            P(None, "rows", "rhs"),
            P(None, None, "rows"),
            P(None, None, ("rows", "rhs")),
            P(),
            P(),
        ),
        out_specs=P(None, "rows", "rhs"),
        check_vma=False,
    )
```

```python
import functools
import jax
import jax.numpy as jnp
from jax import lax
from jax.experimental import pallas as pl
from jax.experimental.pallas import tpu as pltpu
from jax.sharding import PartitionSpec as P

NX, NZ, NC, NY = 4, 8, 2, 4
NB = 1024
HALF = 16
OWN_HINT = 3 * 10**9
MARK_HINT = 2 * 10**9
F32 = jnp.float32
BF16 = jnp.bfloat16


def row_perm(move):
    pairs = []
    for x in range(NX):
        for z in range(NZ):
            for c in range(NC):
                a, b, d = move(x, z, c)
                pairs.append(((x * NZ + z) * NC + c, ((a % NX) * NZ + b % NZ) * NC + d))
    return pairs


def flip_x(v, m):
    return lax.ppermute(v, "rows", row_perm(lambda x, z, c: (x ^ m, z, c))) if m else v


def flip_z(v, m):
    return lax.ppermute(v, "rows", row_perm(lambda x, z, c: (x, z ^ m, c)))


def flip_y(v, m):
    return lax.ppermute(v, "rhs", [(i, i ^ m) for i in range(NY)]) if m else v


X_GROUPS = [[(x * NZ + z) * NC + c for x in range(NX)] for z in range(NZ) for c in range(NC)]


def exchange_x(v):
    return lax.all_to_all(v, "rows", 0, 0, axis_index_groups=X_GROUPS, tiled=True)


def other_core(v):
    return lax.ppermute(v, "rows", row_perm(lambda x, z, c: (x, z, 1 - c)))


def far(*values):
    return [pltpu.with_memory_space_constraint(v, pltpu.HBM) for v in values]


def params(mib):
    return pltpu.CompilerParams(vmem_limit_bytes=mib << 20)


ANY = pl.BlockSpec(memory_space=pl.ANY)


def whole(*shape):
    return pl.BlockSpec(shape, lambda i, s: (0,) * len(shape))


def call(body, name, grid, info, args, in_specs, out_specs, out_shape, mib, scratch=(), hint=0, aliases={}):
    cost = pl.CostEstimate(flops=hint, bytes_accessed=1 << 20, transcendentals=0)
    return pl.pallas_call(
        body,
        grid_spec=pltpu.PrefetchScalarGridSpec(
            num_scalar_prefetch=1,
            grid=(grid,),
            in_specs=in_specs,
            out_specs=out_specs,
            scratch_shapes=list(scratch),
        ),
        out_shape=out_shape,
        input_output_aliases=aliases,
        compiler_params=params(mib),
        cost_estimate=cost if hint else None,
        name=name,
    )(info, *args)


def prep_kernel(start, slabs, diags, *refs):
    outs, (slab, diag, came) = refs[:NX], refs[NX:]
    cycle, x = start[0] // (NX * NZ * NC), lax.axis_index("rows") // (NZ * NC)
    copies = [pltpu.make_async_copy(diags, diag, came.at[4])]
    for i in range(4):
        part = pl.ds(256 * i, 256)
        copies.append(pltpu.make_async_copy(slabs.at[cycle, part], slab.at[part], came.at[i]))
    for copy in copies:
        copy.start()
    copies[0].wait()
    for s in range(NX):
        to = x ^ s
        for level in range(2):
            outs[s][32 + level : 33 + level, :] = diag[level, pl.ds(cycle, 1), :]
            outs[s][34 + level : 35 + level, :] = diag[level, pl.ds(to, 1), :]
        outs[s][36:40, :] = jnp.zeros((4, NB), F32)
    for i in range(4):
        copies[i + 1].wait()
        at = slice(256 * i, 256 * i + 256)
        flipped = slab[at, :].T
        for to in range(NX):
            rows = flipped[32 * to : 32 * to + 32]
            for s in range(NX):

                @pl.when(to ^ s == x)
                def _():
                    outs[s][:32, at] = rows


def prep(start, right_sides, diag):
    return call(
        prep_kernel,
        "prep",
        1,
        start,
        far(right_sides, diag),
        [ANY] * 2,
        [whole(40, NB)] * NX,
        [jax.ShapeDtypeStruct((40, NB), F32)] * NX,
        12,
        [
            pltpu.VMEM((NB, 128), F32),
            pltpu.VMEM((2, 4, NB), F32),
            pltpu.SemaphoreType.DMA((5,)),
        ],
    )


def split(v):
    top = v.astype(BF16)
    return top, (v - top.astype(F32)).astype(BF16)


TOKEN = jax.ShapeDtypeStruct((8, 128), F32)


def split_band_kernel(info, rows, token, top, low, mark, near, near_top, near_low, came, went):
    mark[...] = jnp.zeros((8, 128), F32)
    copies = []
    for i in range(4):
        part = pl.ds(2048 * i, 2048)
        copies.append(pltpu.make_async_copy(rows.at[part], near.at[part], came.at[i]))
        copies[i].start()
    sent = []
    for i in range(4):
        copies[i].wait()
        part = slice(256 * i, 256 * i + 256)
        for c in range(4):
            for half in range(2):
                a, b = split(near[pl.ds(2048 * i + 4 * half + c, 256, stride=8), :])
                at = slice(256 * c + 128 * half, 256 * c + 128 * half + 128)
                near_top[part, at] = a
                near_low[part, at] = b
        part = pl.ds(256 * i, 256)
        for j, (here, there) in enumerate(((near_top, top), (near_low, low))):
            sent.append(pltpu.make_async_copy(here.at[part], there.at[part], went.at[j, i]))
            sent[-1].start()
    for copy in sent:
        copy.wait()


def split_band(info, band_rows, token):
    view = band_rows.reshape(NB, 4, 2, 128).transpose(0, 2, 1, 3).reshape(8 * NB, 128)
    return call(
        split_band_kernel,
        "split_band",
        1,
        info,
        (*far(view), token),
        [ANY] * 2,
        [ANY] * 2 + [whole(8, 128)],
        [pltpu.HBM((NB, NB), BF16)] * 2 + [TOKEN],
        12,
        [
            pltpu.VMEM((8 * NB, 128), F32),
            pltpu.VMEM((NB, NB), BF16),
            pltpu.VMEM((NB, NB), BF16),
            pltpu.SemaphoreType.DMA((4,)),
            pltpu.SemaphoreType.DMA((2, 4)),
        ],
    )


def product(a, b):
    return jnp.dot(a, b, preferred_element_type=F32)


def solve_kernel(info, *refs):
    pieces, inverse = refs[:4], refs[4]
    keep, send, got, near, full, done = refs[6:]
    copies = []
    for i in range(4):
        part = (pl.ds(0, 256 * (i + 1)), pl.ds(256 * i, 256))
        copies.append(pltpu.make_async_copy(inverse.at[part], near.at[part], done.at[i]))
        copies[i].start()
    x, core = info[1], info[3]
    for s in range(NX):
        got[x ^ s] = pieces[s][...]
    x0 = info[0] % (NX * NZ * NC) // (NZ * NC)
    high = x0 & 2
    sign_high = jnp.where(high == 0, 1.0, -1.0).astype(F32)
    sign_low = jnp.where((x0 & 1) == 0, 1.0, -1.0).astype(F32)
    level = [
        got[high | p, 32:33, :] * (got[p, :32, :] + sign_high * got[p + 2, :32, :])
        for p in range(2)
    ]
    top, low = split(got[x0, 33:34, :] * (0.5 * (level[0] + sign_low * level[1])))
    for i in range(4):
        depth, at = 256 * (i + 1), slice(256 * i, 256 * i + 256)
        copies[i].wait()
        a, b = split(near[:depth, at])
        full[:, at] = (
            product(top[:, :depth], b) + product(low[:, :depth], a) + product(top[:, :depth], a)
        )
    keep[...] = full[pl.ds(pl.multiple_of(HALF * core, HALF), HALF), :]
    send[...] = full[pl.ds(pl.multiple_of(HALF * (1 - core), HALF), HALF), :]


def solve(info, pieces, inverse, token):
    return call(
        solve_kernel,
        "solve",
        1,
        info,
        (*pieces, *far(inverse), token),
        [whole(40, NB)] * NX + [ANY] * 2,
        [whole(HALF, NB)] * 2,
        [jax.ShapeDtypeStruct((HALF, NB), F32)] * 2,
        12,
        [
            pltpu.VMEM((NX, 40, NB), F32),
            pltpu.VMEM((NB, NB), F32),
            pltpu.VMEM((32, NB), F32),
            pltpu.SemaphoreType.DMA((4,)),
        ],
        70 * 10**9,
    )


def update_kernel(n, info, *refs):
    own, other = refs[:n], refs[n : 2 * n]
    far_top, far_low = refs[2 * n : 2 * n + 2]
    outs, mine = refs[2 * n + 3 : 3 * n + 3], refs[3 * n + 3]
    left_top, left_low, top, low, done = refs[3 * n + 4 :]
    copies = []
    for c in range(2):
        at = (slice(None), pl.ds(512 * c, 512))
        copies.append(
            [
                pltpu.make_async_copy(far_top.at[at], top.at[at], done.at[0, c]),
                pltpu.make_async_copy(far_low.at[at], low.at[at], done.at[1, c]),
            ]
        )
        for copy in copies[c]:
            copy.start()
    x, core = info[1], info[3]
    for t in range(NX):
        for h in range(NC):
            base = 32 * (x ^ t) + HALF * (core ^ h)
            for s in range(n):
                piece = (other if h else own)[s][HALF * t : HALF * t + HALF, :]
                at = pl.ds(pl.multiple_of(128 * s + base, HALF), HALF)
                left_top[at, :], left_low[at, :] = split(piece)
                if s == 0:
                    mine[pl.ds(pl.multiple_of(base, HALF), HALF), :] = piece
    for c in range(2):
        for copy in copies[c]:
            copy.wait()
        at = slice(512 * c, 512 * c + 512)
        result = (
            product(left_top[...], low[:, at])
            + product(left_low[...], top[:, at])
            + product(left_top[...], top[:, at])
        )
        for s in range(n):
            outs[s][:, at] = result[128 * s : 128 * s + 128]


def update(info, own, other, top, low, token, hint):
    n = len(own)
    return call(
        functools.partial(update_kernel, n),
        "update",
        1,
        info,
        (*own, *other, *far(top, low), token),
        [whole(64, NB)] * (2 * n) + [ANY] * 3,
        [whole(128, NB)] * (n + 1),
        [jax.ShapeDtypeStruct((128, NB), F32)] * (n + 1),
        20,
        [
            pltpu.VMEM((128 * n, NB), BF16),
            pltpu.VMEM((128 * n, NB), BF16),
            pltpu.VMEM((NB, NB), BF16),
            pltpu.VMEM((NB, NB), BF16),
            pltpu.SemaphoreType.DMA((2, 2)),
        ],
        hint,
    )


def mid_kernel(info, *refs):
    got, pieces, outs, mark = refs[0], refs[1:5], refs[6:10], refs[10]
    mark[...] = jnp.zeros((8, 128), F32)
    x = info[1]
    high = [jnp.where((x ^ s) & 2 == 0, 1.0, -1.0).astype(F32) for s in range(NX)]
    low = [jnp.where((x ^ s) & 1 == 0, 1.0, -1.0).astype(F32) for s in range(NX)]
    for i in range(NB // 128):
        at = slice(128 * i, 128 * i + 128)
        scale = [pieces[s][:, at].T for s in range(NX)]
        v = [got[x ^ s, at, :] for s in range(NX)]
        v = [scale[s][:, 2:3] * (v[s ^ 2] + high[s] * v[s]) for s in range(NX)]
        for s in range(NX):
            outs[s][at, :] = (0.5 * scale[s][:, 3:4]) * (v[s ^ 1] + low[s] * v[s])


def mid(info, got, pieces, token):
    return call(
        mid_kernel,
        "mid",
        1,
        info,
        (got, *far(*pieces), token),
        [whole(NX, NB, 128)]
        + [pl.BlockSpec((8, NB), lambda i, s: (4, 0))] * NX
        + [ANY],
        [whole(NB, 128)] * NX + [whole(8, 128)],
        [jax.ShapeDtypeStruct((NB, 128), F32)] * NX + [TOKEN],
        12,
        hint=10**10,
    )


def mark_kernel(info, *refs):
    refs[-1][...] = jnp.zeros((8, 128), F32)


def mark_after(info, values, hint):
    return call(
        mark_kernel, "mark", 1, info, values, [ANY] * len(values), whole(8, 128), TOKEN, 4, hint=hint
    )


def block_index(info, step):
    return ((info[1] ^ step) * NX + info[1]) * (NZ * NC) + info[2] * NC + info[3]


def last_kernel(info, *refs):
    moved, mine, parts, out, block, went = refs[:4], refs[4], refs[5:9], *refs[10:]
    start, copies = info[0], []
    for s in range(NX):
        index = block_index(info, s)

        @pl.when(index < start)
        def _():
            block[s] = moved[s][...]

        @pl.when(index > start)
        def _():
            column = pl.ds(pl.multiple_of(256 * (info[1] ^ s), 256), 256)
            for q in range(NY):
                at = pl.ds(pl.multiple_of(256 * (info[4] ^ q), 256), 256)
                block[s, at, :] = moved[s][at, :] - parts[q][:, column].T

        @pl.when(index == start)
        def _():
            block[s] = mine[...].T

        copies.append(pltpu.make_async_copy(block.at[s], out.at[info[1] ^ s], went.at[s]))
        copies[s].start()
    for copy in copies:
        copy.wait()


def last(info, moved, mine, parts, token):
    return call(
        last_kernel,
        "last",
        1,
        info,
        (*moved, mine, *parts, token),
        [whole(NB, 128)] * NX + [whole(128, NB)] * (NY + 1) + [ANY],
        ANY,
        pltpu.HBM((4, NB, 128), F32),
        12,
        [pltpu.VMEM((4, NB, 128), F32), pltpu.SemaphoreType.DMA((4,))],
    )


def after(value, token):
    return lax.optimization_barrier((value, token))[0]


def per_device(right_sides, butterfly_diagonals, band_rows, diag_inverse, band_block):
    place = lax.axis_index("rows")
    y = lax.axis_index("rhs")
    x, z, core = place // (NZ * NC), place // NC % NZ, place % NC
    start = band_block[0]
    info = jnp.stack([start, x, z, core, y]).astype(jnp.int32)
    z0 = start % (NX * NZ * NC) // NC % NZ
    core0 = start % NC

    message = prep(band_block, right_sides, butterfly_diagonals)
    pieces = [flip_x(message[s], s) for s in range(NX)]
    top, low, ready = split_band(info, band_rows, message[0])
    mixed = exchange_x(after(right_sides, ready))

    half, other_half = solve(info, pieces, diag_inverse, ready)
    half = jnp.where(core == core0, half, other_core(other_half))

    away = z ^ z0
    got = [flip_z(half, m) for m in (1, 2, 3)]
    for m in (1, 2, 3):
        half = jnp.where(away == m, got[m - 1], half)
    half = jnp.where(away >= 4, flip_z(half, 6), half)

    *blocks, mixed_done = mid(info, mixed, pieces, half)
    line = [half] + [after(flip_x(half, t), mixed_done) for t in range(1, NX)]
    line = jnp.concatenate(line, axis=0)

    one, three = flip_y(line, 1), flip_y(line, 3)
    cross = [other_core(v) for v in (one, three)]
    two = flip_y(after(line, (one, three)), 2)
    one, three, token = update(info, [one, three], cross, top, low, mixed_done, 1)
    blocks[2] = after(blocks[2], token)
    moved = [flip_x(v, s) for s, v in enumerate(blocks)]
    two = after(two, token)
    token = mark_after(info, [moved[1], moved[3], token], MARK_HINT)
    two, token = update(info, [two], [other_core(two)], top, low, token, 1)
    zero, mine = update(info, [line], [other_core(line)], top, low, token, 1)
    one, three = flip_y(one, 1), flip_y(three, 3)
    token = mark_after(info, [one, three, zero], OWN_HINT)
    return last(info, moved, mine, [zero, one, flip_y(two, 2), three], token)


def solution(mesh):
    return jax.shard_map(
        per_device,
        mesh=mesh,
        in_specs=(
            P(None, "rows", "rhs"),
            P(None, None, "rows"),
            P(None, None, ("rows", "rhs")),
            P(),
            P(),
        ),
        out_specs=P(None, "rows", "rhs"),
        check_vma=False,
    )
```

```python
import functools
import jax
import jax.numpy as jnp
from jax import lax
from jax.experimental import pallas as pl
from jax.experimental.pallas import tpu as pltpu
from jax.sharding import PartitionSpec as P

NX, NZ, NC, NY = 4, 8, 2, 4
NB = 1024
HALF = 16
OWN_HINT = 3 * 10**9
MARK_HINT = 2 * 10**9
F32 = jnp.float32
BF16 = jnp.bfloat16


def row_perm(move):
    pairs = []
    for x in range(NX):
        for z in range(NZ):
            for c in range(NC):
                a, b, d = move(x, z, c)
                pairs.append(((x * NZ + z) * NC + c, ((a % NX) * NZ + b % NZ) * NC + d))
    return pairs


def flip_x(v, m):
    return lax.ppermute(v, "rows", row_perm(lambda x, z, c: (x ^ m, z, c))) if m else v


def flip_z(v, m):
    return lax.ppermute(v, "rows", row_perm(lambda x, z, c: (x, z ^ m, c)))


def flip_y(v, m):
    return lax.ppermute(v, "rhs", [(i, i ^ m) for i in range(NY)]) if m else v


X_GROUPS = [[(x * NZ + z) * NC + c for x in range(NX)] for z in range(NZ) for c in range(NC)]


def exchange_x(v):
    return lax.all_to_all(v, "rows", 0, 0, axis_index_groups=X_GROUPS, tiled=True)


def other_core(v):
    return lax.ppermute(v, "rows", row_perm(lambda x, z, c: (x, z, 1 - c)))


def far(*values):
    return [pltpu.with_memory_space_constraint(v, pltpu.HBM) for v in values]


def params(mib):
    return pltpu.CompilerParams(vmem_limit_bytes=mib << 20)


ANY = pl.BlockSpec(memory_space=pl.ANY)


def whole(*shape):
    return pl.BlockSpec(shape, lambda i, s: (0,) * len(shape))


def call(body, name, grid, info, args, in_specs, out_specs, out_shape, mib, scratch=(), hint=0, aliases={}):
    cost = pl.CostEstimate(flops=hint, bytes_accessed=1 << 20, transcendentals=0)
    return pl.pallas_call(
        body,
        grid_spec=pltpu.PrefetchScalarGridSpec(
            num_scalar_prefetch=1,
            grid=(grid,),
            in_specs=in_specs,
            out_specs=out_specs,
            scratch_shapes=list(scratch),
        ),
        out_shape=out_shape,
        input_output_aliases=aliases,
        compiler_params=params(mib),
        cost_estimate=cost if hint else None,
        name=name,
    )(info, *args)


def prep_kernel(start, slabs, diags, keep, send, slab, diag, came):
    cycle, core = start[0] // (NX * NZ * NC), lax.axis_index("rows") % NC
    copies = [pltpu.make_async_copy(diags, diag, came.at[4])]
    for i in range(4):
        part = pl.ds(256 * i, 256)
        copies.append(pltpu.make_async_copy(slabs.at[cycle, part], slab.at[part], came.at[i]))
    for copy in copies:
        copy.start()
    copies[0].wait()
    for out in (keep, send):
        for level in range(2):
            out[64 + level : 65 + level, :] = diag[level, pl.ds(cycle, 1), :]
        out[66:72, :] = jnp.zeros((6, NB), F32)
    for i in range(4):
        copies[i + 1].wait()
        at = slice(256 * i, 256 * i + 256)
        flipped = slab[at, :].T
        for to in range(NX):
            first, second = [flipped[HALF * j : HALF * j + HALF] for j in (2 * to, 2 * to + 1)]
            rows = slice(HALF * to, HALF * to + HALF)
            keep[rows, at] = jnp.where(core == 0, first, second)
            send[rows, at] = jnp.where(core == 0, second, first)


def prep(start, right_sides, diag):
    return call(
        prep_kernel,
        "prep",
        1,
        start,
        far(right_sides, diag),
        [ANY] * 2,
        [whole(72, NB)] * 2,
        [jax.ShapeDtypeStruct((72, NB), F32)] * 2,
        12,
        [
            pltpu.VMEM((NB, 128), F32),
            pltpu.VMEM((2, 4, NB), F32),
            pltpu.SemaphoreType.DMA((5,)),
        ],
    )


def pack_kernel(info, keep, came, diag, *outs):
    x = info[1]
    for source, mine in ((keep, True), (came, False)):

        @pl.when((info[3] == info[0] % NC) == mine)
        def _():
            for s in range(NX):
                at = pl.ds(pl.multiple_of(HALF * (x ^ s), HALF), HALF)
                outs[s][:16, :] = source[at, :]
                outs[s][16:18, :] = source[64:66, :]

    for s in range(NX):
        for level in range(2):
            outs[s][18 + level : 19 + level, :] = diag[level, pl.ds(x ^ s, 1), :]
        outs[s][20:24, :] = jnp.zeros((4, NB), F32)


def pack(info, keep, came, diag):
    return call(
        pack_kernel,
        "pack",
        1,
        info,
        (keep, came, diag),
        [whole(72, NB)] * 2 + [whole(2, 4, NB)],
        [whole(24, NB)] * NX,
        [jax.ShapeDtypeStruct((24, NB), F32)] * NX,
        8,
    )


def split(v):
    top = v.astype(BF16)
    return top, (v - top.astype(F32)).astype(BF16)


TOKEN = jax.ShapeDtypeStruct((8, 128), F32)


def split_band_kernel(info, rows, token, top, low):
    for c in range(4):
        for half in range(2):
            a, b = split(rows[pl.ds(4 * half + c, NB, stride=8), :])
            at = slice(256 * c + 128 * half, 256 * c + 128 * half + 128)
            top[:, at] = a
            low[:, at] = b


def split_band(info, band_rows, token):
    view = band_rows.reshape(NB, 4, 2, 128).transpose(0, 2, 1, 3).reshape(8 * NB, 128)
    return call(
        split_band_kernel,
        "split_band",
        1,
        info,
        (view, token),
        [whole(8 * NB, 128), ANY],
        [whole(NB, NB)] * 2,
        [jax.ShapeDtypeStruct((NB, NB), BF16)] * 2,
        12,
        hint=10**9,
    )


def product(a, b):
    return jnp.dot(a, b, preferred_element_type=F32)


def solve_kernel(info, *refs):
    pieces, inverse = refs[:4], refs[4]
    out, got, near, done = refs[5:]
    copies = []
    for i in range(4):
        part = (pl.ds(0, 256 * (i + 1)), pl.ds(256 * i, 256))
        copies.append(pltpu.make_async_copy(inverse.at[part], near.at[part], done.at[i]))
        copies[i].start()
    x = info[1]
    for s in range(NX):
        got[x ^ s] = pieces[s][...]
    x0 = info[0] % (NX * NZ * NC) // (NZ * NC)
    high = x0 & 2
    sign_high = jnp.where(high == 0, 1.0, -1.0).astype(F32)
    sign_low = jnp.where((x0 & 1) == 0, 1.0, -1.0).astype(F32)
    level = [
        got[high | p, 16:17, :] * (got[p, :16, :] + sign_high * got[p + 2, :16, :])
        for p in range(2)
    ]
    top, low = split(got[x0, 17:18, :] * (0.5 * (level[0] + sign_low * level[1])))
    for i in range(4):
        depth, at = 256 * (i + 1), slice(256 * i, 256 * i + 256)
        copies[i].wait()
        a, b = split(near[:depth, at])
        out[:, at] = (
            product(top[:, :depth], b) + product(low[:, :depth], a) + product(top[:, :depth], a)
        )


def solve(info, pieces, inverse):
    return call(
        solve_kernel,
        "solve",
        1,
        info,
        (*pieces, *far(inverse)),
        [whole(24, NB)] * NX + [ANY],
        whole(HALF, NB),
        jax.ShapeDtypeStruct((HALF, NB), F32),
        12,
        [
            pltpu.VMEM((NX, 24, NB), F32),
            pltpu.VMEM((NB, NB), F32),
            pltpu.SemaphoreType.DMA((4,)),
        ],
        70 * 10**9,
    )


def update_kernel(n, info, *refs):
    own, other = refs[:n], refs[n : 2 * n]
    top, low = refs[2 * n : 2 * n + 2]
    outs, mine = refs[2 * n + 3 : 3 * n + 3], refs[3 * n + 3]
    left_top, left_low = refs[3 * n + 4 :]
    x, core = info[1], info[3]
    for t in range(NX):
        for h in range(NC):
            base = 32 * (x ^ t) + HALF * (core ^ h)
            for s in range(n):
                piece = (other if h else own)[s][HALF * t : HALF * t + HALF, :]
                at = pl.ds(pl.multiple_of(128 * s + base, HALF), HALF)
                left_top[at, :], left_low[at, :] = split(piece)
                if s == 0:
                    mine[pl.ds(pl.multiple_of(base, HALF), HALF), :] = piece
    for c in range(2):
        at = slice(512 * c, 512 * c + 512)
        result = (
            product(left_top[...], low[:, at])
            + product(left_low[...], top[:, at])
            + product(left_top[...], top[:, at])
        )
        for s in range(n):
            outs[s][:, at] = result[128 * s : 128 * s + 128]


def update(info, own, other, top, low, token, hint):
    n = len(own)
    return call(
        functools.partial(update_kernel, n),
        "update",
        1,
        info,
        (*own, *other, top, low, token),
        [whole(64, NB)] * (2 * n) + [whole(NB, NB)] * 2 + [ANY],
        [whole(128, NB)] * (n + 1),
        [jax.ShapeDtypeStruct((128, NB), F32)] * (n + 1),
        16,
        [pltpu.VMEM((128 * n, NB), BF16)] * 2,
        hint,
    )


def mid_kernel(info, *refs):
    got, pieces, outs, mark = refs[0], refs[1:5], refs[6:10], refs[10]
    mark[...] = jnp.zeros((8, 128), F32)
    x = info[1]
    high = [jnp.where((x ^ s) & 2 == 0, 1.0, -1.0).astype(F32) for s in range(NX)]
    low = [jnp.where((x ^ s) & 1 == 0, 1.0, -1.0).astype(F32) for s in range(NX)]
    for i in range(NB // 128):
        at = slice(128 * i, 128 * i + 128)
        scale = [pieces[s][:, at].T for s in range(NX)]
        v = [got[x ^ s, at, :] for s in range(NX)]
        v = [scale[s][:, 2:3] * (v[s ^ 2] + high[s] * v[s]) for s in range(NX)]
        for s in range(NX):
            outs[s][at, :] = (0.5 * scale[s][:, 3:4]) * (v[s ^ 1] + low[s] * v[s])


def mid(info, got, pieces, token):
    return call(
        mid_kernel,
        "mid",
        1,
        info,
        (got, *far(*pieces), token),
        [whole(NX, NB, 128)]
        + [pl.BlockSpec((8, NB), lambda i, s: (2, 0))] * NX
        + [ANY],
        [whole(NB, 128)] * NX + [whole(8, 128)],
        [jax.ShapeDtypeStruct((NB, 128), F32)] * NX + [TOKEN],
        12,
        hint=10**10,
    )


def mark_kernel(info, *refs):
    refs[-1][...] = jnp.zeros((8, 128), F32)


def mark_after(info, values, hint):
    return call(
        mark_kernel, "mark", 1, info, values, [ANY] * len(values), whole(8, 128), TOKEN, 4, hint=hint
    )


def block_index(info, step):
    return ((info[1] ^ step) * NX + info[1]) * (NZ * NC) + info[2] * NC + info[3]


def last_kernel(info, *refs):
    moved, mine, parts, out, block, went = refs[:4], refs[4], refs[5:9], *refs[10:]
    start, copies = info[0], []
    for s in range(NX):
        index = block_index(info, s)

        @pl.when(index < start)
        def _():
            block[s] = moved[s][...]

        @pl.when(index > start)
        def _():
            column = pl.ds(pl.multiple_of(256 * (info[1] ^ s), 256), 256)
            for q in range(NY):
                at = pl.ds(pl.multiple_of(256 * (info[4] ^ q), 256), 256)
                block[s, at, :] = moved[s][at, :] - parts[q][:, column].T

        @pl.when(index == start)
        def _():
            block[s] = mine[...].T

        copies.append(pltpu.make_async_copy(block.at[s], out.at[info[1] ^ s], went.at[s]))
        copies[s].start()
    for copy in copies:
        copy.wait()


def last(info, moved, mine, parts, token):
    return call(
        last_kernel,
        "last",
        1,
        info,
        (*moved, mine, *parts, token),
        [whole(NB, 128)] * NX + [whole(128, NB)] * (NY + 1) + [ANY],
        ANY,
        pltpu.HBM((4, NB, 128), F32),
        12,
        [pltpu.VMEM((4, NB, 128), F32), pltpu.SemaphoreType.DMA((4,))],
    )


def after(value, token):
    return lax.optimization_barrier((value, token))[0]


def per_device(right_sides, butterfly_diagonals, band_rows, diag_inverse, band_block):
    place = lax.axis_index("rows")
    y = lax.axis_index("rhs")
    x, z, core = place // (NZ * NC), place // NC % NZ, place % NC
    start = band_block[0]
    info = jnp.stack([start, x, z, core, y]).astype(jnp.int32)
    z0 = start % (NX * NZ * NC) // NC % NZ

    keep, send = prep(band_block, right_sides, butterfly_diagonals)
    message = pack(info, keep, other_core(send), butterfly_diagonals)
    pieces = [flip_x(message[s], s) for s in range(NX)]
    mixed = exchange_x(after(right_sides, message[0]))
    half = solve(info, pieces, diag_inverse)

    away = z ^ z0
    got = [flip_z(half, m) for m in (1, 2, 3)]
    for m in (1, 2, 3):
        half = jnp.where(away == m, got[m - 1], half)
    half = jnp.where(away >= 4, flip_z(half, 6), half)

    *blocks, mixed_done = mid(info, mixed, pieces, half)
    line = [half] + [after(flip_x(half, t), mixed_done) for t in range(1, NX)]
    line = jnp.concatenate(line, axis=0)
    top, low = split_band(info, band_rows, line)

    one, three = flip_y(line, 1), flip_y(line, 3)
    cross = [other_core(after(v, top)) for v in (one, three)]
    two = flip_y(after(line, (one, three)), 2)
    one, three, token = update(info, [one, three], cross, top, low, mixed_done, 1)
    blocks[2] = after(blocks[2], token)
    moved = [flip_x(v, s) for s, v in enumerate(blocks)]
    two = after(two, token)
    token = mark_after(info, [moved[1], moved[3], token], MARK_HINT)
    two, token = update(info, [two], [other_core(two)], top, low, token, 1)
    zero, mine = update(info, [line], [other_core(line)], top, low, token, 1)
    one, three = flip_y(one, 1), flip_y(three, 3)
    token = mark_after(info, [one, three, zero], OWN_HINT)
    return last(info, moved, mine, [zero, one, flip_y(two, 2), three], token)


def solution(mesh):
    return jax.shard_map(
        per_device,
        mesh=mesh,
        in_specs=(
            P(None, "rows", "rhs"),
            P(None, None, "rows"),
            P(None, None, ("rows", "rhs")),
            P(),
            P(),
        ),
        out_specs=P(None, "rows", "rhs"),
        check_vma=False,
    )
```

```python
import functools
import jax
import jax.numpy as jnp
from jax import lax
from jax.experimental import pallas as pl
from jax.experimental.pallas import tpu as pltpu
from jax.sharding import PartitionSpec as P

NX, NZ, NC, NY = 4, 8, 2, 4
NB = 1024
HALF = 16
OWN_HINT = 3 * 10**9
MARK_HINT = 2 * 10**9
F32 = jnp.float32
BF16 = jnp.bfloat16


def row_perm(move):
    pairs = []
    for x in range(NX):
        for z in range(NZ):
            for c in range(NC):
                a, b, d = move(x, z, c)
                pairs.append(((x * NZ + z) * NC + c, ((a % NX) * NZ + b % NZ) * NC + d))
    return pairs


def flip_x(v, m):
    return lax.ppermute(v, "rows", row_perm(lambda x, z, c: (x ^ m, z, c))) if m else v


def flip_z(v, m):
    return lax.ppermute(v, "rows", row_perm(lambda x, z, c: (x, z ^ m, c)))


def flip_y(v, m):
    return lax.ppermute(v, "rhs", [(i, i ^ m) for i in range(NY)]) if m else v


X_GROUPS = [[(x * NZ + z) * NC + c for x in range(NX)] for z in range(NZ) for c in range(NC)]


def exchange_x(v):
    return lax.all_to_all(v, "rows", 0, 0, axis_index_groups=X_GROUPS, tiled=True)


def other_core(v):
    return lax.ppermute(v, "rows", row_perm(lambda x, z, c: (x, z, 1 - c)))


def far(*values):
    return [pltpu.with_memory_space_constraint(v, pltpu.HBM) for v in values]


def params(mib):
    return pltpu.CompilerParams(vmem_limit_bytes=mib << 20)


ANY = pl.BlockSpec(memory_space=pl.ANY)


def whole(*shape):
    return pl.BlockSpec(shape, lambda i, s: (0,) * len(shape))


def call(body, name, grid, info, args, in_specs, out_specs, out_shape, mib, scratch=(), hint=0, aliases={}):
    cost = pl.CostEstimate(flops=hint, bytes_accessed=1 << 20, transcendentals=0)
    return pl.pallas_call(
        body,
        grid_spec=pltpu.PrefetchScalarGridSpec(
            num_scalar_prefetch=1,
            grid=(grid,),
            in_specs=in_specs,
            out_specs=out_specs,
            scratch_shapes=list(scratch),
        ),
        out_shape=out_shape,
        input_output_aliases=aliases,
        compiler_params=params(mib),
        cost_estimate=cost if hint else None,
        name=name,
    )(info, *args)


def prep_kernel(start, slabs, diags, keep, send, slab, diag, came):
    cycle, core = start[0] // (NX * NZ * NC), lax.axis_index("rows") % NC
    copies = [pltpu.make_async_copy(diags, diag, came.at[4])]
    for i in range(4):
        part = pl.ds(256 * i, 256)
        copies.append(pltpu.make_async_copy(slabs.at[cycle, part], slab.at[part], came.at[i]))
    for copy in copies:
        copy.start()
    copies[0].wait()
    for out in (keep, send):
        for level in range(2):
            out[64 + level : 65 + level, :] = diag[level, pl.ds(cycle, 1), :]
        out[66:72, :] = jnp.zeros((6, NB), F32)
    for i in range(4):
        copies[i + 1].wait()
        at = slice(256 * i, 256 * i + 256)
        flipped = slab[at, :].T
        for to in range(NX):
            first, second = [flipped[HALF * j : HALF * j + HALF] for j in (2 * to, 2 * to + 1)]
            rows = slice(HALF * to, HALF * to + HALF)
            keep[rows, at] = jnp.where(core == 0, first, second)
            send[rows, at] = jnp.where(core == 0, second, first)


def prep(start, right_sides, diag):
    return call(
        prep_kernel,
        "prep",
        1,
        start,
        far(right_sides, diag),
        [ANY] * 2,
        [whole(72, NB)] * 2,
        [jax.ShapeDtypeStruct((72, NB), F32)] * 2,
        12,
        [
            pltpu.VMEM((NB, 128), F32),
            pltpu.VMEM((2, 4, NB), F32),
            pltpu.SemaphoreType.DMA((5,)),
        ],
    )


def pack_kernel(info, keep, came, diag, *outs):
    x = info[1]
    for source, mine in ((keep, True), (came, False)):

        @pl.when((info[3] == info[0] % NC) == mine)
        def _():
            for s in range(NX):
                at = pl.ds(pl.multiple_of(HALF * (x ^ s), HALF), HALF)
                outs[s][:16, :] = source[at, :]
                outs[s][16:18, :] = source[64:66, :]

    for s in range(NX):
        for level in range(2):
            outs[s][18 + level : 19 + level, :] = diag[level, pl.ds(x ^ s, 1), :]
        outs[s][20:24, :] = jnp.zeros((4, NB), F32)


def pack(info, keep, came, diag):
    return call(
        pack_kernel,
        "pack",
        1,
        info,
        (keep, came, diag),
        [whole(72, NB)] * 2 + [whole(2, 4, NB)],
        [whole(24, NB)] * NX,
        [jax.ShapeDtypeStruct((24, NB), F32)] * NX,
        8,
    )


def split(v):
    top = v.astype(BF16)
    return top, (v - top.astype(F32)).astype(BF16)


TOKEN = jax.ShapeDtypeStruct((8, 128), F32)


def split_band_kernel(info, rows, token, top, low):
    for c in range(4):
        for half in range(2):
            a, b = split(rows[pl.ds(4 * half + c, NB, stride=8), :])
            at = slice(256 * c + 128 * half, 256 * c + 128 * half + 128)
            top[:, at] = a
            low[:, at] = b


def split_band(info, band_rows, token):
    view = band_rows.reshape(NB, 4, 2, 128).transpose(0, 2, 1, 3).reshape(8 * NB, 128)
    return call(
        split_band_kernel,
        "split_band",
        1,
        info,
        (view, token),
        [whole(8 * NB, 128), ANY],
        [whole(NB, NB)] * 2,
        [jax.ShapeDtypeStruct((NB, NB), BF16)] * 2,
        12,
        hint=10**9,
    )


def product(a, b):
    return jnp.dot(a, b, preferred_element_type=F32)


def solve_kernel(info, *refs):
    pieces, inverse = refs[:4], refs[4]
    out, got, near, done = refs[5:]
    copies = []
    for i in range(4):
        part = (pl.ds(0, 256 * (i + 1)), pl.ds(256 * i, 256))
        copies.append(pltpu.make_async_copy(inverse.at[part], near.at[part], done.at[i]))
        copies[i].start()
    x = info[1]
    for s in range(NX):
        got[x ^ s] = pieces[s][...]
    x0 = info[0] % (NX * NZ * NC) // (NZ * NC)
    high = x0 & 2
    sign_high = jnp.where(high == 0, 1.0, -1.0).astype(F32)
    sign_low = jnp.where((x0 & 1) == 0, 1.0, -1.0).astype(F32)
    level = [
        got[high | p, 16:17, :] * (got[p, :16, :] + sign_high * got[p + 2, :16, :])
        for p in range(2)
    ]
    top, low = split(got[x0, 17:18, :] * (0.5 * (level[0] + sign_low * level[1])))
    for i in range(4):
        depth, at = 256 * (i + 1), slice(256 * i, 256 * i + 256)
        copies[i].wait()
        a, b = split(near[:depth, at])
        out[:, at] = (
            product(top[:, :depth], b) + product(low[:, :depth], a) + product(top[:, :depth], a)
        )


def solve(info, pieces, inverse):
    return call(
        solve_kernel,
        "solve",
        1,
        info,
        (*pieces, *far(inverse)),
        [whole(24, NB)] * NX + [ANY],
        whole(HALF, NB),
        jax.ShapeDtypeStruct((HALF, NB), F32),
        12,
        [
            pltpu.VMEM((NX, 24, NB), F32),
            pltpu.VMEM((NB, NB), F32),
            pltpu.SemaphoreType.DMA((4,)),
        ],
        70 * 10**9,
    )


def update_kernel(n, info, *refs):
    own, other = refs[:n], refs[n : 2 * n]
    top, low = refs[2 * n : 2 * n + 2]
    outs, mine = refs[2 * n + 3 : 3 * n + 3], refs[3 * n + 3]
    left_top, left_low = refs[3 * n + 4 :]
    x, core = info[1], info[3]
    for t in range(NX):
        for h in range(NC):
            base = 32 * (x ^ t) + HALF * (core ^ h)
            for s in range(n):
                piece = (other if h else own)[s][HALF * t : HALF * t + HALF, :]
                at = pl.ds(pl.multiple_of(128 * s + base, HALF), HALF)
                left_top[at, :], left_low[at, :] = split(piece)
                if s == 0:
                    mine[pl.ds(pl.multiple_of(base, HALF), HALF), :] = piece
    for c in range(2):
        at = slice(512 * c, 512 * c + 512)
        result = (
            product(left_top[...], low[:, at])
            + product(left_low[...], top[:, at])
            + product(left_top[...], top[:, at])
        )
        for s in range(n):
            outs[s][:, at] = result[128 * s : 128 * s + 128]


def update(info, own, other, top, low, token, hint):
    n = len(own)
    return call(
        functools.partial(update_kernel, n),
        "update",
        1,
        info,
        (*own, *other, top, low, token),
        [whole(64, NB)] * (2 * n) + [whole(NB, NB)] * 2 + [ANY],
        [whole(128, NB)] * (n + 1),
        [jax.ShapeDtypeStruct((128, NB), F32)] * (n + 1),
        16,
        [pltpu.VMEM((128 * n, NB), BF16)] * 2,
        hint,
    )


def mid_kernel(info, *refs):
    got, pieces, outs, mark = refs[0], refs[1:5], refs[6:10], refs[10]
    mark[...] = jnp.zeros((8, 128), F32)
    x = info[1]
    high = [jnp.where((x ^ s) & 2 == 0, 1.0, -1.0).astype(F32) for s in range(NX)]
    low = [jnp.where((x ^ s) & 1 == 0, 1.0, -1.0).astype(F32) for s in range(NX)]
    for i in range(NB // 128):
        at = slice(128 * i, 128 * i + 128)
        scale = [pieces[s][:, at].T for s in range(NX)]
        v = [got[x ^ s, at, :] for s in range(NX)]
        v = [scale[s][:, 2:3] * (v[s ^ 2] + high[s] * v[s]) for s in range(NX)]
        for s in range(NX):
            outs[s][at, :] = (0.5 * scale[s][:, 3:4]) * (v[s ^ 1] + low[s] * v[s])


def mid(info, got, pieces, token):
    return call(
        mid_kernel,
        "mid",
        1,
        info,
        (got, *far(*pieces), token),
        [whole(NX, NB, 128)]
        + [pl.BlockSpec((8, NB), lambda i, s: (2, 0))] * NX
        + [ANY],
        [whole(NB, 128)] * NX + [whole(8, 128)],
        [jax.ShapeDtypeStruct((NB, 128), F32)] * NX + [TOKEN],
        12,
        hint=10**10,
    )


def mark_kernel(info, *refs):
    refs[-1][...] = jnp.zeros((8, 128), F32)


def mark_after(info, values, hint):
    return call(
        mark_kernel, "mark", 1, info, values, [ANY] * len(values), whole(8, 128), TOKEN, 4, hint=hint
    )


def block_index(info, step):
    return ((info[1] ^ step) * NX + info[1]) * (NZ * NC) + info[2] * NC + info[3]


def quarter(info, q):
    return pl.ds(pl.multiple_of(256 * (info[4] ^ q), 256), 256)


def columns(info, s):
    return pl.ds(pl.multiple_of(256 * (info[1] ^ s), 256), 256)


NEAR = (0, 1, 3)


def send(copies, source, out, done):
    copies.append(pltpu.make_async_copy(source, out, done))
    copies[-1].start()


def subtract_kernel(info, *refs):
    moved, mine, parts, (out, block, went) = refs[:3], refs[3], refs[4:7], refs[7:]
    start, copies = info[0], []
    for j, s in enumerate(NEAR):
        index = block_index(info, s)

        @pl.when(index < start)
        def _():
            block[j] = moved[j][...]

        @pl.when(index > start)
        def _():
            for part, q in zip(parts, NEAR):
                at = quarter(info, q)
                block[j, at, :] = moved[j][at, :] - part[:, columns(info, s)].T

        @pl.when(index == start)
        def _():
            block[j] = mine[...].T

        for i, q in enumerate(NEAR):
            at = quarter(info, q)
            send(copies, block.at[j, at], out.at[info[1] ^ s, at], went.at[j, i])
    for copy in copies:
        copy.wait()


def subtract(info, moved, mine, parts):
    return call(
        subtract_kernel,
        "subtract",
        1,
        info,
        (*moved, mine, *parts),
        [whole(NB, 128)] * 3 + [whole(128, NB)] * 4,
        ANY,
        pltpu.HBM((4, NB, 128), F32),
        12,
        [pltpu.VMEM((3, NB, 128), F32), pltpu.SemaphoreType.DMA((3, 3))],
        OWN_HINT,
    )


def last_kernel(info, before, *refs):
    moved, mine, parts, (out, block, went) = refs[:4], refs[4], refs[5:9], refs[9:]
    start, copies = info[0], []
    for s in (2, 0, 1, 3):
        index = block_index(info, s)
        quarters = range(NY) if s == 2 else (2,)
        for q in quarters:
            at = quarter(info, q)

            @pl.when(index < start)
            def _():
                block[s, at, :] = moved[s][at, :]

            @pl.when(index > start)
            def _():
                block[s, at, :] = moved[s][at, :] - parts[q][:, columns(info, s)].T

            @pl.when(index == start)
            def _():
                block[s, at, :] = mine[:, at].T

            send(copies, block.at[s, at], out.at[info[1] ^ s, at], went.at[s, q])
    for copy in copies:
        copy.wait()


def last(info, before, moved, mine, parts):
    return call(
        last_kernel,
        "last",
        1,
        info,
        (before, *moved, mine, *parts),
        [ANY] + [whole(NB, 128)] * 4 + [whole(128, NB)] * (NY + 1),
        ANY,
        pltpu.HBM((4, NB, 128), F32),
        12,
        [pltpu.VMEM((4, NB, 128), F32), pltpu.SemaphoreType.DMA((4, 4))],
        aliases={1: 0},
    )


def after(value, token):
    return lax.optimization_barrier((value, token))[0]


def per_device(right_sides, butterfly_diagonals, band_rows, diag_inverse, band_block):
    place = lax.axis_index("rows")
    y = lax.axis_index("rhs")
    x, z, core = place // (NZ * NC), place // NC % NZ, place % NC
    start = band_block[0]
    info = jnp.stack([start, x, z, core, y]).astype(jnp.int32)
    z0 = start % (NX * NZ * NC) // NC % NZ

    keep, send = prep(band_block, right_sides, butterfly_diagonals)
    message = pack(info, keep, other_core(send), butterfly_diagonals)
    pieces = [flip_x(message[s], s) for s in range(NX)]
    mixed = exchange_x(after(right_sides, message[0]))
    half = solve(info, pieces, diag_inverse)

    away = z ^ z0
    got = [flip_z(half, m) for m in (1, 2, 3)]
    for m in (1, 2, 3):
        half = jnp.where(away == m, got[m - 1], half)
    half = jnp.where(away >= 4, flip_z(half, 6), half)

    *blocks, mixed_done = mid(info, mixed, pieces, half)
    line = [half] + [after(flip_x(half, t), mixed_done) for t in range(1, NX)]
    line = jnp.concatenate(line, axis=0)
    top, low = split_band(info, band_rows, line)

    one, three = flip_y(line, 1), flip_y(line, 3)
    cross = [other_core(after(v, top)) for v in (one, three)]
    two = flip_y(after(line, (one, three)), 2)
    one, three, token = update(info, [one, three], cross, top, low, mixed_done, 1)
    blocks[2] = after(blocks[2], token)
    moved = [flip_x(v, s) for s, v in enumerate(blocks)]
    two = after(two, token)
    token = mark_after(info, [moved[1], moved[3], token], MARK_HINT)
    two, token = update(info, [two], [other_core(two)], top, low, token, 1)
    zero, mine = update(info, [line], [other_core(line)], top, low, token, 1)
    one, three = flip_y(one, 1), flip_y(three, 3)
    before = subtract(info, [moved[i] for i in NEAR], mine, [zero, one, three])
    return last(info, before, moved, mine, [zero, one, flip_y(two, 2), three])


def solution(mesh):
    return jax.shard_map(
        per_device,
        mesh=mesh,
        in_specs=(
            P(None, "rows", "rhs"),
            P(None, None, "rows"),
            P(None, None, ("rows", "rhs")),
            P(),
            P(),
        ),
        out_specs=P(None, "rows", "rhs"),
        check_vma=False,
    )
```

```python
import functools
import jax
import jax.numpy as jnp
from jax import lax
from jax.experimental import pallas as pl
from jax.experimental.pallas import tpu as pltpu
from jax.sharding import PartitionSpec as P

NX, NZ, NC, NY = 4, 8, 2, 4
NB = 1024
HALF = 16
OWN_HINT = 3 * 10**9
MARK_HINT = 2 * 10**9
F32 = jnp.float32
BF16 = jnp.bfloat16


def row_perm(move):
    pairs = []
    for x in range(NX):
        for z in range(NZ):
            for c in range(NC):
                a, b, d = move(x, z, c)
                pairs.append(((x * NZ + z) * NC + c, ((a % NX) * NZ + b % NZ) * NC + d))
    return pairs


def flip_x(v, m):
    return lax.ppermute(v, "rows", row_perm(lambda x, z, c: (x ^ m, z, c))) if m else v


def flip_z(v, m):
    return lax.ppermute(v, "rows", row_perm(lambda x, z, c: (x, z ^ m, c)))


def flip_y(v, m):
    return lax.ppermute(v, "rhs", [(i, i ^ m) for i in range(NY)]) if m else v


X_GROUPS = [[(x * NZ + z) * NC + c for x in range(NX)] for z in range(NZ) for c in range(NC)]


def exchange_x(v):
    return lax.all_to_all(v, "rows", 0, 0, axis_index_groups=X_GROUPS, tiled=True)


def other_core(v):
    return lax.ppermute(v, "rows", row_perm(lambda x, z, c: (x, z, 1 - c)))


def far(*values):
    return [pltpu.with_memory_space_constraint(v, pltpu.HBM) for v in values]


def params(mib):
    return pltpu.CompilerParams(vmem_limit_bytes=mib << 20)


ANY = pl.BlockSpec(memory_space=pl.ANY)


def whole(*shape):
    return pl.BlockSpec(shape, lambda i, s: (0,) * len(shape))


def call(body, name, grid, info, args, in_specs, out_specs, out_shape, mib, scratch=(), hint=0, aliases={}):
    cost = pl.CostEstimate(flops=hint, bytes_accessed=1 << 20, transcendentals=0)
    return pl.pallas_call(
        body,
        grid_spec=pltpu.PrefetchScalarGridSpec(
            num_scalar_prefetch=1,
            grid=(grid,),
            in_specs=in_specs,
            out_specs=out_specs,
            scratch_shapes=list(scratch),
        ),
        out_shape=out_shape,
        input_output_aliases=aliases,
        compiler_params=params(mib),
        cost_estimate=cost if hint else None,
        name=name,
    )(info, *args)


def prep_kernel(start, slabs, diags, keep, send, slab, diag, came):
    cycle, core = start[0] // (NX * NZ * NC), lax.axis_index("rows") % NC
    copies = [pltpu.make_async_copy(diags, diag, came.at[4])]
    for i in range(4):
        part = pl.ds(256 * i, 256)
        copies.append(pltpu.make_async_copy(slabs.at[cycle, part], slab.at[part], came.at[i]))
    for copy in copies:
        copy.start()
    copies[0].wait()
    for out in (keep, send):
        for level in range(2):
            out[64 + level : 65 + level, :] = diag[level, pl.ds(cycle, 1), :]
        out[66:72, :] = jnp.zeros((6, NB), F32)
    for i in range(4):
        copies[i + 1].wait()
        at = slice(256 * i, 256 * i + 256)
        flipped = slab[at, :].T
        for to in range(NX):
            first, second = [flipped[HALF * j : HALF * j + HALF] for j in (2 * to, 2 * to + 1)]
            rows = slice(HALF * to, HALF * to + HALF)
            keep[rows, at] = jnp.where(core == 0, first, second)
            send[rows, at] = jnp.where(core == 0, second, first)


def prep(start, right_sides, diag):
    return call(
        prep_kernel,
        "prep",
        1,
        start,
        far(right_sides, diag),
        [ANY] * 2,
        [whole(72, NB)] * 2,
        [jax.ShapeDtypeStruct((72, NB), F32)] * 2,
        12,
        [
            pltpu.VMEM((NB, 128), F32),
            pltpu.VMEM((2, 4, NB), F32),
            pltpu.SemaphoreType.DMA((5,)),
        ],
    )


def pack_kernel(info, keep, came, diag, *outs):
    x = info[1]
    for source, mine in ((keep, True), (came, False)):

        @pl.when((info[3] == info[0] % NC) == mine)
        def _():
            for s in range(NX):
                at = pl.ds(pl.multiple_of(HALF * (x ^ s), HALF), HALF)
                outs[s][:16, :] = source[at, :]
                outs[s][16:18, :] = source[64:66, :]

    for s in range(NX):
        for level in range(2):
            outs[s][18 + level : 19 + level, :] = diag[level, pl.ds(x ^ s, 1), :]
        outs[s][20:24, :] = jnp.zeros((4, NB), F32)


def pack(info, keep, came, diag):
    return call(
        pack_kernel,
        "pack",
        1,
        info,
        (keep, came, diag),
        [whole(72, NB)] * 2 + [whole(2, 4, NB)],
        [whole(24, NB)] * NX,
        [jax.ShapeDtypeStruct((24, NB), F32)] * NX,
        8,
    )


def split(v):
    top = v.astype(BF16)
    return top, (v - top.astype(F32)).astype(BF16)


TOKEN = jax.ShapeDtypeStruct((8, 128), F32)


def split_band_kernel(info, rows, token, top, low):
    for c in range(4):
        for half in range(2):
            a, b = split(rows[pl.ds(4 * half + c, NB, stride=8), :])
            at = slice(256 * c + 128 * half, 256 * c + 128 * half + 128)
            top[:, at] = a
            low[:, at] = b


def split_band(info, band_rows, token):
    view = band_rows.reshape(NB, 4, 2, 128).transpose(0, 2, 1, 3).reshape(8 * NB, 128)
    return call(
        split_band_kernel,
        "split_band",
        1,
        info,
        (view, token),
        [whole(8 * NB, 128), ANY],
        [whole(NB, NB)] * 2,
        [jax.ShapeDtypeStruct((NB, NB), BF16)] * 2,
        12,
        hint=10**9,
    )


def product(a, b):
    return jnp.dot(a, b, preferred_element_type=F32)


def solve_kernel(info, *refs):
    pieces, inverse = refs[:4], refs[4]
    out, got, near, done = refs[5:]
    copies = []
    for i in range(4):
        copies.append([])
        for j in range(i + 1):
            part = (pl.ds(256 * j, 256), pl.ds(256 * i, 256))
            copies[i].append(
                pltpu.make_async_copy(inverse.at[part], near.at[part], done.at[i, j])
            )
            copies[i][j].start()
    x = info[1]
    for s in range(NX):
        got[x ^ s] = pieces[s][...]
    x0 = info[0] % (NX * NZ * NC) // (NZ * NC)
    high = x0 & 2
    sign_high = jnp.where(high == 0, 1.0, -1.0).astype(F32)
    sign_low = jnp.where((x0 & 1) == 0, 1.0, -1.0).astype(F32)
    level = [
        got[high | p, 16:17, :] * (got[p, :16, :] + sign_high * got[p + 2, :16, :])
        for p in range(2)
    ]
    top, low = split(got[x0, 17:18, :] * (0.5 * (level[0] + sign_low * level[1])))
    for i in range(4):
        depth, at = 256 * (i + 1), slice(256 * i, 256 * i + 256)
        for copy in copies[i]:
            copy.wait()
        a, b = split(near[:depth, at])
        out[:, at] = (
            product(top[:, :depth], b) + product(low[:, :depth], a) + product(top[:, :depth], a)
        )


def solve(info, pieces, inverse):
    return call(
        solve_kernel,
        "solve",
        1,
        info,
        (*pieces, *far(inverse)),
        [whole(24, NB)] * NX + [ANY],
        whole(HALF, NB),
        jax.ShapeDtypeStruct((HALF, NB), F32),
        12,
        [
            pltpu.VMEM((NX, 24, NB), F32),
            pltpu.VMEM((NB, NB), F32),
            pltpu.SemaphoreType.DMA((4, 4)),
        ],
        70 * 10**9,
    )


def update_kernel(n, info, *refs):
    own, other = refs[:n], refs[n : 2 * n]
    top, low = refs[2 * n : 2 * n + 2]
    outs, mine = refs[2 * n + 3 : 3 * n + 3], refs[3 * n + 3]
    left_top, left_low = refs[3 * n + 4 :]
    x, core = info[1], info[3]
    for t in range(NX):
        for h in range(NC):
            base = 32 * (x ^ t) + HALF * (core ^ h)
            for s in range(n):
                piece = (other if h else own)[s][HALF * t : HALF * t + HALF, :]
                at = pl.ds(pl.multiple_of(128 * s + base, HALF), HALF)
                left_top[at, :], left_low[at, :] = split(piece)
                if s == 0:
                    mine[pl.ds(pl.multiple_of(base, HALF), HALF), :] = piece
    for c in range(2):
        at = slice(512 * c, 512 * c + 512)
        result = (
            product(left_top[...], low[:, at])
            + product(left_low[...], top[:, at])
            + product(left_top[...], top[:, at])
        )
        for s in range(n):
            outs[s][:, at] = result[128 * s : 128 * s + 128]


def update(info, own, other, top, low, token, hint):
    n = len(own)
    return call(
        functools.partial(update_kernel, n),
        "update",
        1,
        info,
        (*own, *other, top, low, token),
        [whole(64, NB)] * (2 * n) + [whole(NB, NB)] * 2 + [ANY],
        [whole(128, NB)] * (n + 1),
        [jax.ShapeDtypeStruct((128, NB), F32)] * (n + 1),
        16,
        [pltpu.VMEM((128 * n, NB), BF16)] * 2,
        hint,
    )


def mid_kernel(info, *refs):
    got, pieces, outs, mark = refs[0], refs[1:5], refs[6:10], refs[10]
    mark[...] = jnp.zeros((8, 128), F32)
    x = info[1]
    high = [jnp.where((x ^ s) & 2 == 0, 1.0, -1.0).astype(F32) for s in range(NX)]
    low = [jnp.where((x ^ s) & 1 == 0, 1.0, -1.0).astype(F32) for s in range(NX)]
    for i in range(NB // 128):
        at = slice(128 * i, 128 * i + 128)
        scale = [pieces[s][:, at].T for s in range(NX)]
        v = [got[x ^ s, at, :] for s in range(NX)]
        v = [scale[s][:, 2:3] * (v[s ^ 2] + high[s] * v[s]) for s in range(NX)]
        for s in range(NX):
            outs[s][at, :] = (0.5 * scale[s][:, 3:4]) * (v[s ^ 1] + low[s] * v[s])


def mid(info, got, pieces, token):
    return call(
        mid_kernel,
        "mid",
        1,
        info,
        (got, *far(*pieces), token),
        [whole(NX, NB, 128)]
        + [pl.BlockSpec((8, NB), lambda i, s: (2, 0))] * NX
        + [ANY],
        [whole(NB, 128)] * NX + [whole(8, 128)],
        [jax.ShapeDtypeStruct((NB, 128), F32)] * NX + [TOKEN],
        12,
        hint=10**10,
    )


def mark_kernel(info, *refs):
    refs[-1][...] = jnp.zeros((8, 128), F32)


def mark_after(info, values, hint):
    return call(
        mark_kernel, "mark", 1, info, values, [ANY] * len(values), whole(8, 128), TOKEN, 4, hint=hint
    )


def block_index(info, step):
    return ((info[1] ^ step) * NX + info[1]) * (NZ * NC) + info[2] * NC + info[3]


def quarter(info, q):
    return pl.ds(pl.multiple_of(256 * (info[4] ^ q), 256), 256)


def columns(info, s):
    return pl.ds(pl.multiple_of(256 * (info[1] ^ s), 256), 256)


NEAR = (0, 1, 3)


def send(copies, source, out, done):
    copies.append(pltpu.make_async_copy(source, out, done))
    copies[-1].start()


def subtract_kernel(info, *refs):
    moved, mine, parts, (out, block, went) = refs[:3], refs[3], refs[4:7], refs[7:]
    start, copies = info[0], []
    for j, s in enumerate(NEAR):
        index = block_index(info, s)

        @pl.when(index < start)
        def _():
            block[j] = moved[j][...]

        @pl.when(index > start)
        def _():
            for part, q in zip(parts, NEAR):
                at = quarter(info, q)
                block[j, at, :] = moved[j][at, :] - part[:, columns(info, s)].T

        @pl.when(index == start)
        def _():
            block[j] = mine[...].T

        for i, q in enumerate(NEAR):
            at = quarter(info, q)
            send(copies, block.at[j, at], out.at[info[1] ^ s, at], went.at[j, i])
    for copy in copies:
        copy.wait()


def subtract(info, moved, mine, parts):
    return call(
        subtract_kernel,
        "subtract",
        1,
        info,
        (*moved, mine, *parts),
        [whole(NB, 128)] * 3 + [whole(128, NB)] * 4,
        ANY,
        pltpu.HBM((4, NB, 128), F32),
        12,
        [pltpu.VMEM((3, NB, 128), F32), pltpu.SemaphoreType.DMA((3, 3))],
        OWN_HINT,
    )


def last_kernel(info, before, *refs):
    moved, mine, parts, (out, block, went) = refs[:4], refs[4], refs[5:9], refs[9:]
    start, copies = info[0], []
    for s in (2, 0, 1, 3):
        index = block_index(info, s)
        quarters = range(NY) if s == 2 else (2,)
        for q in quarters:
            at = quarter(info, q)

            @pl.when(index < start)
            def _():
                block[s, at, :] = moved[s][at, :]

            @pl.when(index > start)
            def _():
                block[s, at, :] = moved[s][at, :] - parts[q][:, columns(info, s)].T

            @pl.when(index == start)
            def _():
                block[s, at, :] = mine[:, at].T

            send(copies, block.at[s, at], out.at[info[1] ^ s, at], went.at[s, q])
    for copy in copies:
        copy.wait()


def last(info, before, moved, mine, parts):
    return call(
        last_kernel,
        "last",
        1,
        info,
        (before, *moved, mine, *parts),
        [ANY] + [whole(NB, 128)] * 4 + [whole(128, NB)] * (NY + 1),
        ANY,
        pltpu.HBM((4, NB, 128), F32),
        12,
        [pltpu.VMEM((4, NB, 128), F32), pltpu.SemaphoreType.DMA((4, 4))],
        aliases={1: 0},
    )


def after(value, token):
    return lax.optimization_barrier((value, token))[0]


def per_device(right_sides, butterfly_diagonals, band_rows, diag_inverse, band_block):
    place = lax.axis_index("rows")
    y = lax.axis_index("rhs")
    x, z, core = place // (NZ * NC), place // NC % NZ, place % NC
    start = band_block[0]
    info = jnp.stack([start, x, z, core, y]).astype(jnp.int32)
    z0 = start % (NX * NZ * NC) // NC % NZ

    keep, send = prep(band_block, right_sides, butterfly_diagonals)
    message = pack(info, keep, other_core(send), butterfly_diagonals)
    pieces = [flip_x(message[s], s) for s in range(NX)]
    mixed = exchange_x(after(right_sides, message[0]))
    half = solve(info, pieces, diag_inverse)

    away = z ^ z0
    got = [flip_z(half, m) for m in (1, 2, 3)]
    for m in (1, 2, 3):
        half = jnp.where(away == m, got[m - 1], half)
    half = jnp.where(away >= 4, flip_z(half, 6), half)

    *blocks, mixed_done = mid(info, mixed, pieces, half)
    line = [half] + [after(flip_x(half, t), mixed_done) for t in range(1, NX)]
    line = jnp.concatenate(line, axis=0)
    top, low = split_band(info, band_rows, line)

    one, three = flip_y(line, 1), flip_y(line, 3)
    cross = [other_core(after(v, top)) for v in (one, three)]
    two = flip_y(after(line, (one, three)), 2)
    one, three, token = update(info, [one, three], cross, top, low, mixed_done, 1)
    blocks[2] = after(blocks[2], token)
    moved = [flip_x(v, s) for s, v in enumerate(blocks)]
    two = after(two, token)
    token = mark_after(info, [moved[1], moved[3], token], MARK_HINT)
    two, token = update(info, [two], [other_core(two)], top, low, token, 1)
    zero, mine = update(info, [line], [other_core(line)], top, low, token, 1)
    one, three = flip_y(one, 1), flip_y(three, 3)
    before = subtract(info, [moved[i] for i in NEAR], mine, [zero, one, three])
    return last(info, before, moved, mine, [zero, one, flip_y(two, 2), three])


def solution(mesh):
    return jax.shard_map(
        per_device,
        mesh=mesh,
        in_specs=(
            P(None, "rows", "rhs"),
            P(None, None, "rows"),
            P(None, None, ("rows", "rhs")),
            P(),
            P(),
        ),
        out_specs=P(None, "rows", "rhs"),
        check_vma=False,
    )
```
